256 devices in a mesh: seq: 32 (over z_lo, y, x), dp: 8 (over z_hi, core).
Axes of the slice: x: 4, y: 4, z: 8 (z_hi: 4, z_lo: 2; z = z_hi * 2 + z_lo), core: 2. Of those that a mesh axis runs over, the one named last changes fastest.
Arguments:
- query_rows: bfloat16 [8, 4096, 4096], P('dp', 'seq'), may hold values from -6 to 6
- key_rows: bfloat16 [8, 4096, 4096], P('dp', 'seq'), may hold values from -6 to 6
- value_rows: bfloat16 [8, 4096, 4096], P('dp', 'seq'), may hold values from -6 to 6
- cotangent: bfloat16 [8, 4096, 4096], P('dp', 'seq'), may hold values from -6 to 6
- short_filter: float32 [3, 3, 4096], replicated, may hold values from -3 to 3
- residue: float32 [4096, 16], P('seq'), may hold values from -1.5 to 1.5
- decay_rate: float32 [4096, 16], P('seq'), as said below
Outputs:
- query_grad: bfloat16 [8, 4096, 4096], P('dp', 'seq')
- key_grad: bfloat16 [8, 4096, 4096], P('dp', 'seq')
- value_grad: bfloat16 [8, 4096, 4096], P('dp', 'seq')
- short_grad: float32 [3, 3, 4096], replicated
- residue_grad: float32 [4096, 16], P('seq')
- decay_grad: float32 [4096, 16], P('seq')
The draws below stay inside these ranges and needn't reach their ends.
Inputs may be any that keep to these rules, and one draw needn't show every extreme that they name: `decay_rate`: every rate lies between 1 / 40960 and 1 / 32.
All inputs are finite; a program needn't handle non-finite values.
Results may differ from the reference program's by a relative error of at most 0.012.
Values may be sent and summed in bfloat16 or wider, within the bound.
No kernel may reach another device: no remote copies, remote signals or barrier semaphores. Data moves between devices by JAX's collectives and lax.ppermute only.
A program may use at most 128 MiB of HBM per device.

```python
import math
import jax
import jax.numpy as jnp
from jax import lax

D = 4096
ORDER = 16
TAPS = 3
SEQLEN = 4096
BATCH = 8


def draw_decay_rate(key, part):
    key = jax.random.fold_in(key, 7)
    first_key, second_key = jax.random.split(key)
    pick = jax.random.uniform(first_key, (D, ORDER), jnp.float32)
    spot = jax.random.uniform(second_key, (D, ORDER), jnp.float32)
    lowest = jnp.log(0.1 / SEQLEN)
    middle = jnp.log(2.0 / SEQLEN)
    highest = jnp.log(1.0 / 32.0)
    share = 0.5
    slower = lowest + spot * (middle - lowest)
    faster = middle + spot * (highest - middle)
    return jnp.exp(jnp.where(pick < share, slower, faster)).astype(jnp.float32)


def shard_levels(own_key, extent, cuts, least, top_value):
    loudness, own = 1.0, jax.random.fold_in(own_key, 6)
    for position, blocks in cuts:
        steps = jnp.exp(jax.random.uniform(jax.random.fold_in(own, position), (blocks,), jnp.float32, least / len(cuts), top_value / len(cuts)))
        loudness = loudness * jnp.repeat(steps, extent[position] // blocks).reshape([-1 if axis == position else 1 for axis in range(len(extent))])
    return loudness


def scatter_about(rng, dims, scale, reach, shards=(), kind=jnp.bfloat16):
    array = jax.random.normal(rng, dims, jnp.float32) * scale
    if len(shards) > 0:
        array = shard_levels(rng, dims, shards, -0.22, 0.18) * array
    return jnp.clip(array, min=-reach, max=reach).astype(kind)


def setup_inputs(seed: int = 0) -> dict:
    splits = jax.random.split(jax.random.key(seed), 8)
    query_rows = scatter_about(splits[0], (BATCH, SEQLEN, D), 1.0, 6.0, ((0, 8), (1, 32)))
    key_rows = scatter_about(splits[1], (BATCH, SEQLEN, D), 1.0, 6.0, ((0, 8), (1, 32)))
    value_rows = scatter_about(splits[2], (BATCH, SEQLEN, D), 1.0, 6.0, ((0, 8), (1, 32)))
    cotangent = scatter_about(splits[3], (BATCH, SEQLEN, D), 1.0, 6.0, ((0, 8), (1, 32)))
    short_filter = scatter_about(splits[4], (3, TAPS, D), 0.5, 3.0, (), jnp.float32)
    residue = scatter_about(splits[5], (D, ORDER), 0.25, 1.5, ((0, 32),), jnp.float32)
    decay_rate = draw_decay_rate(jax.random.fold_in(splits[7], 71), 0)
    return dict(query_rows=query_rows, key_rows=key_rows, value_rows=value_rows, cotangent=cotangent, short_filter=short_filter, residue=residue, decay_rate=decay_rate)


def decay_filter(residue, decay_rate, length):
    times = jnp.arange(length).astype(residue.dtype)
    weights = residue * jnp.sqrt(-jnp.expm1(-2.0 * decay_rate))

    def add_mode(total, pair):
        amount, speed = pair
        return (total + amount[None, :] * jnp.exp(-speed[None, :] * times[:, None]), 0)
    start = jnp.zeros((length, residue.shape[0]), residue.dtype)
    impulse, unused = lax.scan(add_mode, start, (weights.T, decay_rate.T))
    return impulse

def round_trip(values):
    return lax.optimization_barrier(values.astype(jnp.bfloat16)).astype(values.dtype)

def block_pass(query_rows, key_rows, value_rows, cotangent, short_filter, residue, decay_rate):
    batch, length, width = query_rows.shape
    margin = short_filter.shape[1] - 1
    inputs = jnp.stack([query_rows, key_rows, value_rows]).astype(short_filter.dtype)
    padded = jnp.pad(inputs, ((0, 0), (0, 0), (margin, 0), (0, 0)))
    shorted = jnp.zeros_like(inputs)
    for offset in range(margin + 1):
        shorted = shorted + short_filter[:, offset][:, None, None, :] * padded[:, :, margin - offset:margin - offset + length, :]
    query_short, key_short, value_short = (shorted[0], shorted[1], shorted[2])
    gated = round_trip(key_short * value_short)
    impulse, pullback = jax.vjp(lambda amount, speed: decay_filter(amount, speed, length), residue, decay_rate)
    points = 2 * length
    spectrum_u = jnp.fft.rfft(gated, points, axis=1)
    spectrum_h = jnp.fft.rfft(impulse, points, axis=0)[None]
    mixed = round_trip(jnp.fft.irfft(spectrum_u * spectrum_h, points, axis=1)[:, :length])
    upstream = cotangent.astype(short_filter.dtype)
    grad_mixed = round_trip(upstream * query_short)
    spectrum_g = jnp.fft.rfft(grad_mixed, points, axis=1)
    grad_gated = round_trip(jnp.fft.irfft(jnp.conj(spectrum_h) * spectrum_g, points, axis=1)[:, :length])
    grad_impulse = lax.optimization_barrier(jnp.sum(jnp.fft.irfft(spectrum_g * jnp.conj(spectrum_u), points, axis=1)[:, :length], axis=0))
    grad_short = jnp.stack([upstream * mixed, grad_gated * value_short, grad_gated * key_short])
    trailing = jnp.pad(grad_short, ((0, 0), (0, 0), (0, margin), (0, 0)))
    grad_inputs = jnp.zeros_like(grad_short)
    filter_terms = []
    for offset in range(margin + 1):
        grad_inputs = grad_inputs + short_filter[:, offset][:, None, None, :] * trailing[:, :, offset:offset + length, :]
        filter_terms.append(lax.optimization_barrier(jnp.sum(grad_short * padded[:, :, margin - offset:margin - offset + length, :], axis=(1, 2))))
    filter_grad = jnp.stack(filter_terms, axis=1)
    residue_grad, rate_grad = pullback(grad_impulse)
    factor = 1.0 / math.sqrt(batch * length)
    return (grad_inputs[0].astype(jnp.bfloat16), grad_inputs[1].astype(jnp.bfloat16), grad_inputs[2].astype(jnp.bfloat16), filter_grad * factor, residue_grad * factor, decay_rate * rate_grad * factor)

def reference(query_rows, key_rows, value_rows, cotangent, short_filter, residue, decay_rate):
    batch, length, width = query_rows.shape
    block = math.gcd(width, 128)
    count = width // block
    taps = short_filter.shape[1]
    modes = residue.shape[1]

    def to_blocks(values):
        return values.reshape(batch, length, count, block).transpose(2, 0, 1, 3)

    def from_blocks(values):
        return values.transpose(1, 2, 0, 3).reshape(batch, length, width)
    pieces = (to_blocks(query_rows), to_blocks(key_rows), to_blocks(value_rows), to_blocks(cotangent), short_filter.reshape(3, taps, count, block).transpose(2, 0, 1, 3), residue.reshape(count, block, modes), decay_rate.reshape(count, block, modes))

    def one_block(group):
        return block_pass(group[0], group[1], group[2], group[3], group[4], group[5], group[6])
    results = lax.map(one_block, pieces)
    return (from_blocks(results[0]), from_blocks(results[1]), from_blocks(results[2]), results[3].transpose(1, 2, 0, 3).reshape(3, taps, width), results[4].reshape(width, modes), results[5].reshape(width, modes))
```

```python
import math

import jax
import jax.numpy as jnp
import numpy as np
from jax import lax
from jax.experimental import pallas as pl
from jax.experimental.pallas import tpu as pltpu
from jax.sharding import PartitionSpec as P

BLOCK = 128
TERMS = 16
TOP_RATE = 1.0 / 32.0
FREQS = 128
LANES = 128
BF16 = jnp.bfloat16
F32 = jnp.float32
VMEM_LIMIT = 48 * 1024 * 1024


def decay_terms(times):
    points = 64
    theta = (np.arange(points) + 0.5) * np.pi / points
    rates = (np.cos(theta) + 1.0) * TOP_RATE / 2.0
    values = np.exp(-np.asarray(times, np.float64)[:, None] * rates[None, :])
    basis = np.cos(np.arange(TERMS)[None, :] * theta[:, None]) * (2.0 / points)
    basis[:, 0] *= 0.5
    return values @ basis


def halves(table):
    table = np.asarray(table, np.float32)
    high = table.astype(BF16)
    low = (table - high.astype(np.float32)).astype(BF16)
    return high, low


def paired(table):
    return np.concatenate(halves(table), axis=1)


def make_tables():
    t = np.arange(BLOCK)
    angle = 2.0 * np.pi / (2 * FREQS) * (np.arange(FREQS)[:, None] + 0.5) * t[None, :]
    fore = np.concatenate([np.cos(angle), -np.sin(angle)], axis=0)
    back = np.concatenate([np.cos(angle.T), -np.sin(angle.T)], axis=1) / FREQS
    ahead = decay_terms(t)
    behind = decay_terms(BLOCK - t)
    fore_u = paired(np.concatenate([fore, behind.T], axis=0))
    fore_g = paired(np.concatenate([fore, ahead.T], axis=0))
    impulse_high, impulse_low = halves(fore @ ahead)
    impulse = np.concatenate([impulse_high, impulse_high, impulse_low], axis=1)
    taps = np.zeros((8, TERMS))
    taps[:3] = decay_terms([0, 1, -1])
    taps_high, taps_low = halves(taps)
    return dict(
        fore_u=fore_u,
        fore_g=fore_g,
        impulse=impulse,
        back=back.astype(BF16),
        lag=(ahead.T @ back).astype(BF16),
        ahead_t=ahead.T.astype(BF16),
        behind_t=behind.T.astype(BF16),
        ahead=paired(ahead),
        behind=paired(behind),
        taps3=np.concatenate([taps_high, taps_high, taps_low], axis=1),
        taps2=np.concatenate([taps_high, taps_low], axis=1),
        first=[float(x) for x in taps[0]],
        second=[float(x) for x in taps[1]],
    )


def dot(left, right):
    return jnp.dot(left, right, preferred_element_type=F32)


def whole(shape):
    return pl.BlockSpec(shape, lambda *_: (0,) * len(shape))


def lagged(values, before):
    row = lax.broadcasted_iota(jnp.int32, values.shape, 0)
    one = jnp.where(row == 0, before[1:2], pltpu.roll(values, 1, 0))
    two = pltpu.roll(values, 2, 0)
    two = jnp.where(row == 0, before[0:1], jnp.where(row == 1, before[1:2], two))
    return one, two


def leading(values, after):
    count = values.shape[0]
    row = lax.broadcasted_iota(jnp.int32, values.shape, 0)
    one = jnp.where(row == count - 1, after[0:1], pltpu.roll(values, count - 1, 0))
    two = pltpu.roll(values, count - 2, 0)
    two = jnp.where(
        row == count - 2, after[0:1], jnp.where(row == count - 1, after[1:2], two)
    )
    return one, two


def lanes_of(ref, rows):
    return jnp.concatenate([ref[i, rows, :] for i in range(ref.shape[0])], axis=1)


def prep_kernel(weight_ref, rate_ref, basis_ref, slope_ref, loaded_ref, spread_ref):
    weight = weight_ref[...]
    spot = rate_ref[...] * (2.0 / TOP_RATE) - 1.0
    value, older = jnp.ones_like(spot), spot
    slope, older_slope = jnp.zeros_like(spot), jnp.zeros_like(spot)
    rows = []
    for k in range(TERMS):
        basis_ref[k] = value
        slope_ref[k] = slope * (-2.0 / TOP_RATE)
        loaded = value * weight
        loaded_ref[k] = loaded
        rows.append(jnp.sum(loaded, axis=0, keepdims=True))
        if k == 0:
            following, following_slope = spot, jnp.ones_like(spot)
        else:
            following = 2.0 * spot * value - older
            following_slope = 2.0 * value + 2.0 * spot * slope - older_slope
        older, older_slope = value, slope
        value, slope = following, following_slope
    coefs = jnp.concatenate(rows, axis=0)
    high = coefs.astype(BF16)
    low = (coefs - high.astype(F32)).astype(BF16)
    both = jnp.concatenate([high, low], axis=0)
    spread_ref[...] = jnp.broadcast_to(both[None], spread_ref.shape)


def block_kernel(
    query_ref, key_ref, value_ref, cot_ref, filter_ref, before_ref, coefs_ref,
    fore_u_ref, fore_g_ref, impulse_ref, back_ref, lag_ref, ahead_t_ref, behind_t_ref,
    sent_ref, mixed_ref, grad_ref,
):
    taps = filter_ref[...]
    before = before_ref[...]
    query, key, value = (ref[0].astype(F32) for ref in (query_ref, key_ref, value_ref))
    cot = cot_ref[0].astype(F32)
    queries = (query, *lagged(query, before[0:2]))
    keys = (key, *lagged(key, before[2:4]))
    values = (value, *lagged(value, before[4:6]))

    def short(i, inputs):
        return sum(taps[3 * i + j : 3 * i + j + 1] * inputs[j] for j in range(3))

    key_short, value_short = short(1, keys), short(2, values)
    gated = (key_short * value_short).astype(BF16)
    grad_mixed = (cot * short(0, queries)).astype(BF16)
    u = dot(fore_u_ref[...], jnp.concatenate([gated, gated], axis=0))
    g = dot(fore_g_ref[...], jnp.concatenate([grad_mixed, grad_mixed], axis=0))
    coefs = lanes_of(coefs_ref, slice(None))
    h = dot(impulse_ref[...], jnp.concatenate([coefs, coefs[:TERMS]], axis=0))
    ur, ui, gr, gi, hr, hi = (
        x[part * FREQS : (part + 1) * FREQS] for x in (u, g, h) for part in (0, 1)
    )

    def spectrum(real, imag):
        return jnp.concatenate([real.astype(BF16), imag.astype(BF16)], axis=0)

    mixed = dot(back_ref[...], spectrum(ur * hr - ui * hi, ur * hi + ui * hr))
    grad = dot(back_ref[...], spectrum(gr * hr + gi * hi, gi * hr - gr * hi))
    lag = dot(lag_ref[...], spectrum(gr * ur + gi * ui, gi * ur - gr * ui))
    mixed_ref[...] = mixed
    grad_ref[...] = grad
    rows = [u[2 * FREQS :], g[2 * FREQS :], lag]
    sums = []
    for left, inputs, total, table_ref in (
        (cot, queries, mixed, ahead_t_ref),
        (value_short, keys, grad, behind_t_ref),
        (key_short, values, grad, behind_t_ref),
    ):
        for j in range(3):
            product = left * inputs[j]
            rows.append(dot(table_ref[...], product.astype(BF16)))
            sums.append(jnp.sum(product * total, axis=0, keepdims=True))
    sums.append(jnp.zeros((16 - len(sums), sums[0].shape[1]), F32))
    rows.append(jnp.concatenate(sums, axis=0))
    for index, part in enumerate(rows):
        part = part.astype(BF16)
        for i in range(sent_ref.shape[0]):
            sent_ref[i, index * 16 : index * 16 + 16, :] = part[:, i * LANES : (i + 1) * LANES]


def owner_kernel(first, second, moments_ref, basis_ref, slope_ref, loaded_ref, rate_ref, carry_ref, grads_ref, ahead, behind):
    blocks = moments_ref.shape[1]
    modes = rate_ref.shape[0]
    row = lax.broadcasted_iota(jnp.int32, (blocks, LANES), 0)

    def later(x, by):
        return jnp.where(row >= by, pltpu.roll(x, by, 0), 0.0)

    def sooner(x, by):
        return jnp.where(row < blocks - by, pltpu.roll(x, blocks - by, 0), 0.0)

    lag_rows = [jnp.sum(moments_ref[2 * TERMS + k], axis=0, keepdims=True) for k in range(TERMS)]
    first_rows, second_rows = [], []
    for n in range(modes):
        basis = [basis_ref[k, n : n + 1, :] for k in range(TERMS)]
        slope = [slope_ref[k, n : n + 1, :] for k in range(TERMS)]
        state = sum(basis[k] * moments_ref[k] for k in range(TERMS))
        state_slope = sum(slope[k] * moments_ref[k] for k in range(1, TERMS))
        grad = sum(basis[k] * moments_ref[TERMS + k] for k in range(TERMS))
        grad_slope = sum(slope[k] * moments_ref[TERMS + k] for k in range(1, TERMS))
        factor = jnp.exp(-float(BLOCK) * rate_ref[n : n + 1, :])
        forward, forward_slope, backward = later(state, 1), later(state_slope, 1), sooner(grad, 1)
        by = 1
        while by < blocks:
            moved = later(forward, by)
            forward_slope = forward_slope + factor * (
                later(forward_slope, by) + float(BLOCK * by) * moved
            )
            forward = forward + factor * moved
            backward = backward + factor * sooner(backward, by)
            factor = factor * factor
            by *= 2
        ahead[n] = forward
        behind[n] = backward
        first_sum = jnp.sum(forward * grad, axis=0, keepdims=True)
        second_sum = jnp.sum(forward_slope * grad + forward * grad_slope, axis=0, keepdims=True)
        first_rows.append(first_sum + sum(basis[k] * lag_rows[k] for k in range(TERMS)))
        second_rows.append(second_sum + sum(slope[k] * lag_rows[k] for k in range(1, TERMS)))
    grads_ref[...] = jnp.concatenate(first_rows + second_rows, axis=0)
    totals = [moments_ref[12 * TERMS + i] for i in range(9)]
    edge_one, edge_two = 0.0, 0.0
    for k in range(TERMS):
        carry = sum(loaded_ref[k, n : n + 1, :] * ahead[n] for n in range(modes))
        back = sum(loaded_ref[k, n : n + 1, :] * behind[n] for n in range(modes))
        carry_ref[k] = carry
        carry_ref[TERMS + k] = back
        edge_one = edge_one + first[k] * carry
        edge_two = edge_two + second[k] * carry
        for i in range(9):
            totals[i] = totals[i] + (carry if i < 3 else back) * moments_ref[(3 + i) * TERMS + k]
    carry_ref[2 * TERMS] = sooner(edge_one, 1)
    carry_ref[2 * TERMS + 1] = sooner(edge_two, 1)
    for i in range(9):
        total = jnp.sum(totals[i], axis=0, keepdims=True)
        high = total.astype(BF16).astype(F32)
        carry_ref[2 * TERMS + 2 + i] = jnp.broadcast_to(high, (blocks, LANES))
        carry_ref[2 * TERMS + 11 + i] = jnp.broadcast_to(total - high, (blocks, LANES))
    for i in range(2 * TERMS + 20, carry_ref.shape[0]):
        carry_ref[i] = jnp.zeros((blocks, LANES), F32)


def finish_kernel(
    query_ref, key_ref, value_ref, cot_ref, filter_ref, before_ref, after_ref, coefs_ref,
    mixed_ref, grad_ref, carry_ref, ahead_ref, behind_ref, taps3_ref, taps2_ref,
    query_out, key_out, value_out,
):
    taps = filter_ref[...]
    before, after = before_ref[...], after_ref[...]
    query, key, value = (ref[0].astype(F32) for ref in (query_ref, key_ref, value_ref))
    cot = cot_ref[0].astype(F32)

    def tap(i, j):
        return taps[3 * i + j : 3 * i + j + 1]

    def short(i, inputs):
        return sum(tap(i, j) * inputs[j] for j in range(3))

    def rounded(x):
        return x.astype(BF16).astype(F32)

    key_short = short(1, (key, *lagged(key, before[2:4])))
    value_short = short(2, (value, *lagged(value, before[4:6])))

    def short_after(i, inputs):
        last, next_two = inputs[inputs.shape[0] - 2 :], after[2 * i : 2 * i + 2]
        one = jnp.concatenate([last[1:2], next_two[0:1]], axis=0)
        return tap(i, 0) * next_two + tap(i, 1) * one + tap(i, 2) * last

    query_next, key_next, value_next = (
        short_after(i, x) for i, x in enumerate((query, key, value))
    )
    cot_next = after[6:8]
    gated_next = rounded(key_next * value_next)
    grad_mixed_next = rounded(cot_next[0:1] * query_next[0:1])

    ahead = lanes_of(carry_ref, slice(0, TERMS))
    behind = lanes_of(carry_ref, slice(TERMS, 2 * TERMS))
    rest = lanes_of(carry_ref, slice(2 * TERMS, 3 * TERMS)).astype(F32)
    coefs = lanes_of(coefs_ref, slice(None))
    mixed = mixed_ref[...] + dot(ahead_ref[...], jnp.concatenate([ahead, ahead], axis=0))
    grad = grad_ref[...] + dot(behind_ref[...], jnp.concatenate([behind, behind], axis=0))
    impulse = dot(taps3_ref[...], jnp.concatenate([coefs, coefs[:TERMS]], axis=0))
    edge = dot(taps2_ref[...], jnp.concatenate([behind, behind], axis=0))
    mixed_next = rounded(
        jnp.concatenate(
            [
                rest[0:1] + impulse[0:1] * gated_next[0:1],
                rest[1:2] + impulse[0:1] * gated_next[1:2] + impulse[1:2] * gated_next[0:1],
            ],
            axis=0,
        )
    )
    grad_next = rounded(
        jnp.concatenate([edge[0:1], edge[2:3] - grad_mixed_next * impulse[2:3]], axis=0)
    )
    mixed, grad = rounded(mixed), rounded(grad)
    for i, (out_ref, short_grad, after_grad) in enumerate(
        (
            (query_out, cot * mixed, cot_next * mixed_next),
            (key_out, grad * value_short, grad_next * value_next),
            (value_out, grad * key_short, grad_next * key_next),
        )
    ):
        one, two = leading(short_grad, after_grad)
        out_ref[0] = (tap(i, 0) * short_grad + tap(i, 1) * one + tap(i, 2) * two).astype(BF16)


def body(query_rows, key_rows, value_rows, cotangent, short_filter, residue, decay_rate):
    width = query_rows.shape[2]
    blocks = lax.axis_size("seq")
    groups = lax.axis_size("dp")
    modes = residue.shape[1]
    length = BLOCK * blocks
    wide = min(512, width)
    parts = wide // LANES
    grid = (width // wide,)
    tables = make_tables()
    first, second = tables.pop("first"), tables.pop("second")
    tables = {name: jnp.asarray(table) for name, table in tables.items()}
    params = pltpu.CompilerParams(vmem_limit_bytes=VMEM_LIMIT)

    edge_last = jnp.concatenate([x[0, BLOCK - 2 :] for x in (query_rows, key_rows, value_rows)], axis=0)
    edge_first = jnp.concatenate([x[0, :2] for x in (query_rows, key_rows, value_rows, cotangent)], axis=0)
    before = lax.ppermute(edge_last, "seq", [(i, i + 1) for i in range(blocks - 1)]).astype(F32)
    after = lax.ppermute(edge_first, "seq", [(i + 1, i) for i in range(blocks - 1)]).astype(F32)
    before = jnp.concatenate([before, jnp.zeros((2, width), F32)], axis=0)

    root = jnp.sqrt(-jnp.expm1(-2.0 * decay_rate))
    weight_t = (residue * root).T
    rate_t = decay_rate.T
    small = jax.ShapeDtypeStruct((TERMS, modes, LANES), F32)
    basis, slope, loaded, spread = pl.pallas_call(
        prep_kernel,
        out_shape=(small, small, small, jax.ShapeDtypeStruct((blocks, 2 * TERMS, LANES), BF16)),
        compiler_params=params,
        name="prep",
    )(weight_t, rate_t)
    coefs = lax.all_to_all(spread, "seq", 0, 0, tiled=True)

    filters = short_filter.reshape(9, width)
    tall = pl.BlockSpec((1, BLOCK, wide), lambda c: (0, 0, c))
    flat = pl.BlockSpec((BLOCK, wide), lambda c: (0, c))
    nine = pl.BlockSpec((9, wide), lambda c: (0, c))
    eight = pl.BlockSpec((8, wide), lambda c: (0, c))

    def chunks(rows):
        return pl.BlockSpec((parts, rows, LANES), lambda c: (c, 0, 0))

    names = ("fore_u", "fore_g", "impulse", "back", "lag", "ahead_t", "behind_t")
    sent, mixed, grad = pl.pallas_call(
        block_kernel,
        grid=grid,
        in_specs=[tall] * 4
        + [nine, eight, chunks(2 * TERMS)]
        + [whole(tables[name].shape) for name in names],
        out_specs=(chunks(13 * TERMS), flat, flat),
        out_shape=(
            jax.ShapeDtypeStruct((blocks, 13 * TERMS, LANES), BF16),
            jax.ShapeDtypeStruct((BLOCK, width), F32),
            jax.ShapeDtypeStruct((BLOCK, width), F32),
        ),
        compiler_params=params,
        name="block",
    )(
        query_rows, key_rows, value_rows, cotangent, filters, before, coefs,
        *[tables[name] for name in names],
    )
    moments = lax.all_to_all(sent, "seq", 0, 0, tiled=True)
    moments = moments.transpose(1, 0, 2).astype(F32)

    carry, sums = pl.pallas_call(
        lambda *refs: owner_kernel(first, second, *refs),
        out_shape=(
            jax.ShapeDtypeStruct((4 * TERMS, blocks, LANES), F32),
            jax.ShapeDtypeStruct((2 * modes, LANES), F32),
        ),
        scratch_shapes=[pltpu.VMEM((modes, blocks, LANES), F32)] * 2,
        compiler_params=params,
        name="owner",
    )(moments, basis, slope, loaded, rate_t)
    carry = lax.all_to_all(carry.astype(BF16).transpose(1, 0, 2), "seq", 0, 0, tiled=True)

    root_t = root.T
    first_sum, second_sum = sums[:modes], sums[modes:]
    residue_local = root_t * first_sum
    rate_local = residue.T * (jnp.exp(-2.0 * rate_t) / root_t * first_sum - root_t * second_sum)
    decay_local = rate_t * rate_local
    begin = 2 * TERMS + 2
    shared = carry[:, begin : begin + 9].astype(F32) + carry[:, begin + 9 : begin + 18].astype(F32)
    local = jnp.concatenate([shared.reshape(9 * blocks, LANES), residue_local, decay_local], axis=0)
    local = local.astype(BF16)
    total = lax.all_to_all(
        jnp.broadcast_to(local[None], (groups, *local.shape)), "dp", 0, 0, tiled=True
    )
    names = ("ahead", "behind", "taps3", "taps2")
    outs = pl.pallas_call(
        finish_kernel,
        grid=grid,
        in_specs=[tall] * 4
        + [nine, eight, eight, chunks(2 * TERMS), flat, flat, chunks(4 * TERMS)]
        + [whole(tables[name].shape) for name in names],
        out_specs=[tall] * 3,
        out_shape=[jax.ShapeDtypeStruct(query_rows.shape, BF16)] * 3,
        compiler_params=params,
        name="finish",
    )(
        query_rows, key_rows, value_rows, cotangent, filters, before, after, coefs, mixed, grad, carry,
        *[tables[name] for name in names],
    )
    factor = 1.0 / math.sqrt(query_rows.shape[0] * groups * length)
    total = jnp.sum(total.astype(F32), axis=0) * factor
    filter_grad = total[: 9 * blocks].reshape(blocks, 3, 3, LANES).transpose(1, 2, 0, 3).reshape(3, 3, width)
    residue_grad = total[9 * blocks : 9 * blocks + modes].T
    decay_grad = total[9 * blocks + modes :].T
    return (*outs, filter_grad, residue_grad, decay_grad)


def solution(mesh):
    rows = P("dp", "seq", None)
    return jax.shard_map(
        body,
        mesh=mesh,
        in_specs=(rows, rows, rows, rows, P(), P("seq", None), P("seq", None)),
        out_specs=(rows, rows, rows, P(), P("seq", None), P("seq", None)),
        check_vma=False,
    )
```

```python
import math

import jax
import jax.numpy as jnp
import numpy as np
from jax import lax
from jax.experimental import pallas as pl
from jax.experimental.pallas import tpu as pltpu
from jax.sharding import PartitionSpec as P

BLOCK = 128
CENTRE = BLOCK // 2
TERMS = 10
SHORT_TERMS = 9
PRODUCTS = 9
SENT_ROWS = 128
EARLY_ROWS = 80
CARRY_ROWS = 48
TOP_RATE = 1.0 / 32.0
FREQS = 128
LANES = 128
BF16 = jnp.bfloat16
F32 = jnp.float32
VMEM_LIMIT = 60 * 1024 * 1024
SMALL_LIMIT = 16 * 1024 * 1024
WIDE = 1024


def decay_terms(times, terms=TERMS):
    points = 64
    theta = (np.arange(points) + 0.5) * np.pi / points
    rates = (np.cos(theta) + 1.0) * TOP_RATE / 2.0
    values = np.exp(-np.asarray(times, np.float64)[:, None] * rates[None, :])
    basis = np.cos(np.arange(terms)[None, :] * theta[:, None]) * (2.0 / points)
    basis[:, 0] *= 0.5
    return values @ basis


def halves(table):
    table = np.asarray(table, np.float32)
    high = table.astype(BF16)
    low = (table - high.astype(np.float32)).astype(BF16)
    return high, low


def paired(table):
    return np.concatenate(halves(table), axis=1)


def make_tables():
    t = np.arange(BLOCK)
    angle = 2.0 * np.pi / (2 * FREQS) * (np.arange(FREQS)[:, None] + 0.5) * t[None, :]
    fore = np.concatenate([np.cos(angle), -np.sin(angle)], axis=0)
    back = np.concatenate([np.cos(angle.T), -np.sin(angle.T)], axis=1) / FREQS
    ahead = decay_terms(t - CENTRE)
    behind = decay_terms(CENTRE - t)
    total = PRODUCTS * SHORT_TERMS
    product = np.zeros((total, PRODUCTS, BLOCK))
    for m in range(PRODUCTS):
        part = decay_terms(t - CENTRE if m < 3 else CENTRE - t, SHORT_TERMS).T
        product[m * SHORT_TERMS : (m + 1) * SHORT_TERMS, m] = part
    late = np.zeros((SENT_ROWS - EARLY_ROWS, 7 * BLOCK))
    high, low = halves(behind.T)
    late[1 : 1 + TERMS, : 2 * BLOCK] = np.concatenate([high, low], axis=1)
    high, low = halves(ahead.T)
    late[1 + TERMS : 1 + 2 * TERMS, 2 * BLOCK : 4 * BLOCK] = np.concatenate([high, low], axis=1)
    late[1 + 2 * TERMS : 1 + 3 * TERMS, 4 * BLOCK : 6 * BLOCK] = ahead.T @ back
    late[0, 6 * BLOCK :] = product[total - 1, PRODUCTS - 1]
    impulse_high, impulse_low = halves(fore @ ahead)
    taps = np.zeros((8, TERMS))
    taps[:3] = decay_terms([-CENTRE, 1 - CENTRE, -1 - CENTRE])
    edge = np.zeros((8, TERMS))
    edge[:2] = decay_terms([-CENTRE, -1 - CENTRE])

    def padded(table, repeat=0):
        out = np.zeros((table.shape[0], 16))
        out[:, :TERMS] = table
        out[:, TERMS : TERMS + repeat] = table[:, :repeat]
        return out

    first, second = decay_terms([-CENTRE, 1 - CENTRE])

    def tripled(table):
        high, low = halves(padded(table))
        return np.concatenate([high, high, low], axis=1)

    return dict(
        product=product[:EARLY_ROWS].reshape(EARLY_ROWS, PRODUCTS * BLOCK).astype(BF16),
        late=late.astype(BF16),
        fore=paired(fore),
        impulse=tripled(fore @ ahead),
        back=back.astype(BF16),
        ahead=paired(padded(ahead, 16 - TERMS)),
        behind=paired(padded(behind, 16 - TERMS)),
        taps=tripled(taps),
        edge=paired(padded(edge, 16 - TERMS)),
        first=[float(x) for x in first],
        second=[float(x) for x in second],
    )


def dot(left, right):
    return jnp.dot(left, right, preferred_element_type=F32)


def whole(shape):
    return pl.BlockSpec(shape, lambda *_: (0,) * len(shape))


def later_rows(values, before, by):
    moved = pltpu.roll(values, by, 0)
    top = moved[:8]
    row = lax.broadcasted_iota(jnp.int32, top.shape, 0)
    for i in range(by):
        top = jnp.where(row == i, before[2 - by + i : 3 - by + i], top)
    return jnp.concatenate([top, moved[8:]], axis=0)


def sooner_rows(values, after):
    count = values.shape[0]
    moved = pltpu.roll(values, count - 1, 0)
    row = lax.broadcasted_iota(jnp.int32, (8, values.shape[1]), 0)
    bottom = jnp.where(row == 7, after, moved[count - 8 :])
    return jnp.concatenate([moved[: count - 8], bottom], axis=0)


def lanes_of(ref, rows):
    return jnp.concatenate([ref[i, rows, :] for i in range(ref.shape[0])], axis=1)


def store_chunks(ref, start, rows):
    rows = rows.astype(BF16)
    for i in range(ref.shape[0]):
        ref[i, start : start + rows.shape[0], :] = rows[:, i * LANES : (i + 1) * LANES]


def edges_kernel(query_ref, key_ref, value_ref, cot_ref, query_end, key_end, value_end, last_ref, first_ref):
    ends = [ref[0].astype(F32)[14:] for ref in (query_end, key_end, value_end)]
    ends.append(jnp.zeros_like(ends[0]))
    last_ref[...] = jnp.concatenate(ends, axis=0)
    starts = [ref[0].astype(F32)[:2] for ref in (query_ref, key_ref, value_ref, cot_ref)]
    first_ref[...] = jnp.concatenate(starts, axis=0)


def prep_kernel(weight_ref, rate_ref, basis_ref, slope_ref, loaded_ref, spread_ref):
    weight, rate = weight_ref[...], rate_ref[...]
    centred = weight * jnp.exp(-float(CENTRE) * rate)
    spot = rate * (2.0 / TOP_RATE) - 1.0
    value, older = jnp.ones_like(spot), spot
    slope, older_slope = jnp.zeros_like(spot), jnp.zeros_like(spot)
    rows = []
    for k in range(TERMS):
        basis_ref[k] = value
        slope_ref[k] = slope * (-2.0 / TOP_RATE)
        loaded_ref[k] = value * weight
        rows.append(jnp.sum(value * centred, axis=0, keepdims=True))
        if k == 0:
            following, following_slope = spot, jnp.ones_like(spot)
        else:
            following = 2.0 * spot * value - older
            following_slope = 2.0 * value + 2.0 * spot * slope - older_slope
        older, older_slope = value, slope
        value, slope = following, following_slope
    rows.append(jnp.zeros((16 - TERMS, LANES), F32))
    coefs = jnp.concatenate(rows, axis=0)
    high = coefs.astype(BF16)
    low = (coefs - high.astype(F32)).astype(BF16)
    both = jnp.concatenate([high, low], axis=0)
    spread_ref[...] = jnp.broadcast_to(both[None], spread_ref.shape)


def block_kernel(
    query_ref, key_ref, value_ref, cot_ref, filter_ref, before_ref, coefs_ref,
    fore_ref, impulse_ref, back_ref, product_ref, late_ref,
    sent_ref, mixed_ref, grad_ref, key_short_ref, value_short_ref, products,
):
    before = before_ref[...]
    query, key, value = (ref[0].astype(F32) for ref in (query_ref, key_ref, value_ref))
    cot = cot_ref[0].astype(F32)

    def lagged(i, x):
        edge = before[2 * i : 2 * i + 2]
        return (x, later_rows(x, edge, 1), later_rows(x, edge, 2))

    def short(i, inputs):
        return sum(filter_ref[i, j : j + 1, :] * inputs[j] for j in range(3))

    queries, keys, values = lagged(0, query), lagged(1, key), lagged(2, value)
    key_short, value_short = short(1, keys), short(2, values)
    key_short_ref[...] = key_short.astype(BF16)
    value_short_ref[...] = value_short.astype(BF16)
    gated = (key_short * value_short).astype(BF16)
    grad_mixed = (cot * short(0, queries)).astype(BF16)
    for i, (left, inputs) in enumerate(((cot, queries), (value_short, keys), (key_short, values))):
        for j in range(3):
            start = (3 * i + j) * BLOCK
            products[start : start + BLOCK, :] = (left * inputs[j]).astype(BF16)

    gated_twice = jnp.concatenate([gated, gated], axis=0)
    grad_twice = jnp.concatenate([grad_mixed, grad_mixed], axis=0)
    u = dot(fore_ref[...], gated_twice)
    g = dot(fore_ref[...], grad_twice)
    coefs = lanes_of(coefs_ref, slice(None))
    h = dot(impulse_ref[...], jnp.concatenate([coefs, coefs[:16]], axis=0))
    ur, ui, gr, gi, hr, hi = (
        x[part * FREQS : (part + 1) * FREQS] for x in (u, g, h) for part in (0, 1)
    )

    def spectrum(real, imag):
        return jnp.concatenate([real.astype(BF16), imag.astype(BF16)], axis=0)

    mixed = dot(back_ref[...], spectrum(ur * hr - ui * hi, ur * hi + ui * hr))
    grad = dot(back_ref[...], spectrum(gr * hr + gi * hi, gi * hr - gr * hi))
    lags = spectrum(gr * ur + gi * ui, gi * ur - gr * ui)
    mixed_ref[...] = mixed.astype(BF16)
    grad_ref[...] = grad.astype(BF16)
    late = dot(
        late_ref[...],
        jnp.concatenate([gated_twice, grad_twice, lags, products[(PRODUCTS - 1) * BLOCK :, :]], axis=0),
    )
    row = lax.broadcasted_iota(jnp.int32, (16, late.shape[1]), 0)
    sums = late[32:48]
    for m in range(PRODUCTS):
        product = products[m * BLOCK : (m + 1) * BLOCK, :].astype(F32)
        local = jnp.sum(product * (mixed if m < 3 else grad), axis=0, keepdims=True)
        sums = jnp.where(row == m, local, sums)
    store_chunks(sent_ref, 0, dot(product_ref[...], products[...]))
    store_chunks(sent_ref, EARLY_ROWS, late[:32])
    store_chunks(sent_ref, EARLY_ROWS + 32, sums)


def owner_kernel(
    first, second, moments_ref, basis_ref, slope_ref, loaded_ref, rate_ref, root_ref, amount_ref,
    carry_ref, message_ref, ahead, behind,
):
    blocks = moments_ref.shape[1]
    modes = rate_ref.shape[0]
    row = lax.broadcasted_iota(jnp.int32, (blocks, LANES), 0)
    sum_u = PRODUCTS * SHORT_TERMS
    sum_g, lag, local = sum_u + TERMS, sum_u + 2 * TERMS, EARLY_ROWS + 32

    def later(x, by):
        return jnp.where(row >= by, pltpu.roll(x, by, 0), 0.0)

    def sooner(x, by):
        return jnp.where(row < blocks - by, pltpu.roll(x, blocks - by, 0), 0.0)

    lag_rows = [jnp.sum(moments_ref[lag + k], axis=0, keepdims=True) for k in range(TERMS)]
    first_rows, second_rows = [], []
    for n in range(modes):
        basis = [basis_ref[k, n : n + 1, :] for k in range(TERMS)]
        slope = [slope_ref[k, n : n + 1, :] for k in range(TERMS)]
        state = sum(basis[k] * moments_ref[sum_u + k] for k in range(TERMS))
        state_slope = sum(slope[k] * moments_ref[sum_u + k] for k in range(1, TERMS))
        grad = sum(basis[k] * moments_ref[sum_g + k] for k in range(TERMS))
        grad_slope = sum(slope[k] * moments_ref[sum_g + k] for k in range(1, TERMS))
        rate = rate_ref[n : n + 1, :]
        half = jnp.exp(-float(CENTRE) * rate)
        factor = half * half
        moved = later(state, 1)
        forward = factor * moved
        forward_slope = factor * (later(state_slope, 1) + float(BLOCK) * moved)
        backward = factor * sooner(grad, 1)
        by = 1
        while by < blocks:
            moved = later(forward, by)
            forward_slope = forward_slope + factor * (
                later(forward_slope, by) + float(BLOCK * by) * moved
            )
            forward = forward + factor * moved
            backward = backward + factor * sooner(backward, by)
            factor = factor * factor
            by *= 2
        ahead[n] = forward
        behind[n] = backward
        first_sum = jnp.sum(forward * grad, axis=0, keepdims=True)
        second_sum = jnp.sum(forward_slope * grad + forward * grad_slope, axis=0, keepdims=True)
        near = half * sum(basis[k] * lag_rows[k] for k in range(TERMS))
        near_slope = half * sum(slope[k] * lag_rows[k] for k in range(1, TERMS))
        first_rows.append(first_sum + near)
        second_rows.append(second_sum + near_slope + float(CENTRE) * near)
    totals = [moments_ref[local + m] for m in range(PRODUCTS)]
    edge_one, edge_two = 0.0, 0.0
    for k in range(TERMS):
        carry = sum(loaded_ref[k, n : n + 1, :] * ahead[n] for n in range(modes))
        back = sum(loaded_ref[k, n : n + 1, :] * behind[n] for n in range(modes))
        for start, value in ((0, carry), (16, back)):
            high = value.astype(BF16)
            carry_ref[start + k] = high
            if k < 16 - TERMS:
                carry_ref[start + TERMS + k] = (value - high.astype(F32)).astype(BF16)
        edge_one = edge_one + first[k] * carry
        edge_two = edge_two + second[k] * carry
        if k < SHORT_TERMS:
            for m in range(PRODUCTS):
                totals[m] = totals[m] + (carry if m < 3 else back) * moments_ref[m * SHORT_TERMS + k]
    carry_ref[32] = sooner(edge_one, 1).astype(BF16)
    carry_ref[33] = sooner(edge_two, 1).astype(BF16)
    root, amount = root_ref[...], amount_ref[...]
    first_sum = jnp.concatenate(first_rows, axis=0)
    second_sum = jnp.concatenate(second_rows, axis=0)
    rate = rate_ref[...]
    steep = amount * (jnp.exp(-2.0 * rate) / root * first_sum - root * second_sum)
    for i in range(34, CARRY_ROWS):
        carry_ref[i] = jnp.zeros((blocks, LANES), BF16)
    rows = [jnp.zeros((2, LANES), F32)]
    rows.extend(jnp.sum(total, axis=0, keepdims=True) for total in totals)
    rows.append(jnp.zeros((14 - PRODUCTS, LANES), F32))
    message = jnp.concatenate([*rows, root * first_sum, rate * steep], axis=0).astype(BF16)
    message_ref[...] = jnp.broadcast_to(message[None], message_ref.shape)


def total_kernel(factor, message_ref, carry_ref, sent_ref, residue_ref, decay_ref):
    total = message_ref[0].astype(F32)
    for i in range(1, message_ref.shape[0]):
        total = total + message_ref[i].astype(F32)
    total = total * factor
    modes = residue_ref.shape[1]
    residue_ref[...] = total[16 : 16 + modes].T
    decay_ref[...] = total[16 + modes :].T
    shared = total[:16]
    for block in range(sent_ref.shape[0]):
        sent_ref[block, :32, :] = carry_ref[block, :32, :]
        sent_ref[block, 32:48, :] = (carry_ref[block, 32:48, :].astype(F32) + shared).astype(BF16)


def finish_kernel(
    cot_ref, query_end, key_end, value_end, filter_ref, after_ref, coefs_ref, key_short_ref, value_short_ref,
    mixed_ref, grad_ref, carry_ref, ahead_ref, behind_ref, edge_ref, taps_ref,
    query_out, key_out, value_out, filter_out,
):
    after = after_ref[...]

    def tap(i, j):
        return filter_ref[i, j : j + 1, :]

    def rounded(x):
        return x.astype(BF16).astype(F32)

    def short_after(i, ref):
        last, following = ref[0].astype(F32)[14:], after[2 * i : 2 * i + 2]
        middle = jnp.concatenate([last[1:2], following[0:1]], axis=0)
        return tap(i, 0) * following + tap(i, 1) * middle + tap(i, 2) * last

    ahead = lanes_of(carry_ref, slice(0, 16))
    behind = lanes_of(carry_ref, slice(16, 32))
    rest = lanes_of(carry_ref, slice(32, 48)).astype(F32)
    for m in range(PRODUCTS):
        filter_out[m // 3, m % 3 : m % 3 + 1, :] = rest[2 + m : 3 + m]
    behind_twice = jnp.concatenate([behind, behind], axis=0)
    mixed = mixed_ref[...].astype(F32) + dot(ahead_ref[...], jnp.concatenate([ahead, ahead], axis=0))
    grad = grad_ref[...].astype(F32) + dot(behind_ref[...], behind_twice)
    mixed, grad = rounded(mixed), rounded(grad)

    coefs = lanes_of(coefs_ref, slice(None))
    impulse = dot(taps_ref[...], jnp.concatenate([coefs, coefs[:16]], axis=0))
    edge = dot(edge_ref[...], behind_twice)
    query_next, key_next, value_next = (
        short_after(i, ref) for i, ref in enumerate((query_end, key_end, value_end))
    )
    gated_next = rounded(key_next * value_next)
    grad_mixed_next = rounded(after[6:7] * query_next[0:1])
    mixed_next = (
        rounded(rest[0:1] + impulse[0:1] * gated_next[0:1]),
        rounded(rest[1:2] + impulse[0:1] * gated_next[1:2] + impulse[1:2] * gated_next[0:1]),
    )
    grad_next = rounded(edge[0:1]), rounded(edge[1:2] - impulse[2:3] * grad_mixed_next)

    cot = cot_ref[0].astype(F32)
    for i, (out_ref, left, right, left_next, right_next) in enumerate(
        (
            (query_out, cot, mixed, after[6:8], mixed_next),
            (key_out, value_short_ref[...].astype(F32), grad, value_next, grad_next),
            (value_out, key_short_ref[...].astype(F32), grad, key_next, grad_next),
        )
    ):
        zero, one, two = (tap(i, j) for j in range(3))
        here = left * right
        following = left_next[0:1] * right_next[0]
        inner = one * here + sooner_rows(two * here, two * following)
        inner_after = one * following + two * (left_next[1:2] * right_next[1])
        out_ref[0] = (zero * here + sooner_rows(inner, inner_after)).astype(BF16)


def body(query_rows, key_rows, value_rows, cotangent, short_filter, residue, decay_rate):
    width = query_rows.shape[2]
    blocks = lax.axis_size("seq")
    groups = lax.axis_size("dp")
    modes = residue.shape[1]
    length = BLOCK * blocks
    wide = min(WIDE, width)
    parts = wide // LANES
    grid = (width // wide,)
    tables = make_tables()
    first, second = tables.pop("first"), tables.pop("second")
    tables = {name: jnp.asarray(table) for name, table in tables.items()}
    params = pltpu.CompilerParams(vmem_limit_bytes=VMEM_LIMIT)
    small_params = pltpu.CompilerParams(vmem_limit_bytes=SMALL_LIMIT)

    def shape(*dims, dtype=F32):
        return jax.ShapeDtypeStruct(dims, dtype)

    top = pl.BlockSpec((1, 16, width), lambda c: (0, 0, 0))
    end = pl.BlockSpec((1, 16, width), lambda c: (0, BLOCK // 16 - 1, 0))
    last, front = pl.pallas_call(
        edges_kernel,
        grid=(1,),
        in_specs=[top] * 4 + [end] * 3,
        out_specs=(whole((8, width)), whole((8, width))),
        out_shape=(shape(8, width), shape(8, width)),
        compiler_params=params,
        name="edges",
    )(query_rows, key_rows, value_rows, cotangent, query_rows, key_rows, value_rows)
    before = lax.ppermute(last, "seq", [(i, i + 1) for i in range(blocks - 1)])
    after = lax.ppermute(front, "seq", [(i + 1, i) for i in range(blocks - 1)])

    root = jnp.sqrt(-jnp.expm1(-2.0 * decay_rate))
    weight_t = (residue * root).T
    rate_t = decay_rate.T
    small = shape(TERMS, modes, LANES)
    basis, slope, loaded, spread = pl.pallas_call(
        prep_kernel,
        out_shape=(small, small, small, shape(blocks, 32, LANES, dtype=BF16)),
        compiler_params=params,
        name="prep",
    )(weight_t, rate_t)
    coefs = lax.all_to_all(spread, "seq", 0, 0, tiled=True)

    tall = pl.BlockSpec((1, BLOCK, wide), lambda c: (0, 0, c))
    tall_end = pl.BlockSpec((1, 16, wide), lambda c: (0, BLOCK // 16 - 1, c))
    filters = pl.BlockSpec((3, 3, wide), lambda c: (0, 0, c))

    def flat(rows):
        return pl.BlockSpec((rows, wide), lambda c: (0, c))

    def chunks(rows):
        return pl.BlockSpec((parts, rows, LANES), lambda c: (c, 0, 0))

    def table_specs(names):
        return [whole(tables[name].shape) for name in names]

    names = ("fore", "impulse", "back", "product", "late")
    half = shape(BLOCK, width, dtype=BF16)
    sent, mixed, grad, key_short, value_short = pl.pallas_call(
        block_kernel,
        grid=grid,
        in_specs=[tall] * 4 + [filters, flat(8), chunks(32)] + table_specs(names),
        out_specs=(chunks(SENT_ROWS), *[flat(BLOCK)] * 4),
        out_shape=(shape(blocks, SENT_ROWS, LANES, dtype=BF16), half, half, half, half),
        scratch_shapes=[pltpu.VMEM((PRODUCTS * BLOCK, wide), BF16)],
        compiler_params=params,
        name="block",
    )(
        query_rows, key_rows, value_rows, cotangent, short_filter, before, coefs,
        *[tables[name] for name in names],
    )
    moments = lax.all_to_all(sent, "seq", 0, 0, tiled=True)
    moments = moments.transpose(1, 0, 2).astype(F32)

    carry, message = pl.pallas_call(
        lambda *refs: owner_kernel(first, second, *refs),
        out_shape=(
            shape(CARRY_ROWS, blocks, LANES, dtype=BF16),
            shape(groups, 16 + 2 * modes, LANES, dtype=BF16),
        ),
        scratch_shapes=[pltpu.VMEM((modes, blocks, LANES), F32)] * 2,
        compiler_params=small_params,
        name="owner",
    )(moments, basis, slope, loaded, rate_t, root.T, residue.T)
    message = lax.all_to_all(message, "dp", 0, 0, tiled=True)
    factor = 1.0 / math.sqrt(query_rows.shape[0] * groups * length)
    sent, residue_grad, decay_grad = pl.pallas_call(
        lambda *refs: total_kernel(factor, *refs),
        out_shape=(shape(blocks, CARRY_ROWS, LANES, dtype=BF16), shape(LANES, modes), shape(LANES, modes)),
        compiler_params=small_params,
        name="total",
    )(message, carry.transpose(1, 0, 2))
    carry = lax.all_to_all(sent, "seq", 0, 0, tiled=True)

    names = ("ahead", "behind", "edge", "taps")
    *outs, filter_grad = pl.pallas_call(
        finish_kernel,
        grid=grid,
        in_specs=[tall] + [tall_end] * 3 + [filters, flat(8), chunks(32)] + [flat(BLOCK)] * 4
        + [chunks(CARRY_ROWS)] + table_specs(names),
        out_specs=[tall] * 3 + [filters],
        out_shape=[jax.ShapeDtypeStruct(query_rows.shape, BF16)] * 3 + [shape(3, 3, width)],
        compiler_params=params,
        name="finish",
    )(
        cotangent, query_rows, key_rows, value_rows, short_filter, after, coefs, key_short, value_short,
        mixed, grad, carry, *[tables[name] for name in names],
    )
    return (*outs, filter_grad, residue_grad, decay_grad)


def solution(mesh):
    rows = P("dp", "seq", None)
    return jax.shard_map(
        body,
        mesh=mesh,
        in_specs=(rows, rows, rows, rows, P(), P("seq", None), P("seq", None)),
        out_specs=(rows, rows, rows, P(), P("seq", None), P("seq", None)),
        check_vma=False,
    )
```

```python
import math

import jax
import jax.numpy as jnp
import numpy as np
from jax import lax
from jax.experimental import pallas as pl
from jax.experimental.pallas import tpu as pltpu
from jax.sharding import PartitionSpec as P

BLOCK = 128
CENTRE = BLOCK // 2
TERMS = 10
SHORT_TERMS = 9
PRODUCTS = 9
SENT_ROWS = 128
LAG_ROW = PRODUCTS * SHORT_TERMS
SUM_ROW = 96
CARRY_ROWS = 48
TOP_RATE = 1.0 / 32.0
FREQS = 128
LANES = 128
BF16 = jnp.bfloat16
F32 = jnp.float32
VMEM_LIMIT = 63 * 1024 * 1024
FULL_LIMIT = 64 * 1024 * 1024 - 65536
SMALL_LIMIT = 16 * 1024 * 1024
WIDE = 1024
INNER = 256
SKEW = 2
ORDERED = False


def decay_terms(times, terms=TERMS):
    points = 64
    theta = (np.arange(points) + 0.5) * np.pi / points
    rates = (np.cos(theta) + 1.0) * TOP_RATE / 2.0
    values = np.exp(-np.asarray(times, np.float64)[:, None] * rates[None, :])
    basis = np.cos(np.arange(terms)[None, :] * theta[:, None]) * (2.0 / points)
    basis[:, 0] *= 0.5
    return values @ basis


def halves(table):
    table = np.asarray(table, np.float32)
    high = table.astype(BF16)
    low = (table - high.astype(np.float32)).astype(BF16)
    return high, low


def paired(table):
    return np.concatenate(halves(table), axis=1)


def make_tables():
    t = np.arange(BLOCK)
    angle = 2.0 * np.pi / (2 * FREQS) * (np.arange(FREQS)[:, None] + 0.5) * t[None, :]
    fore = np.concatenate([np.cos(angle), -np.sin(angle)], axis=0)
    back = np.concatenate([np.cos(angle.T), -np.sin(angle.T)], axis=1) / FREQS
    ahead = decay_terms(t - CENTRE)
    behind = decay_terms(CENTRE - t)
    moments = np.zeros((SUM_ROW, (PRODUCTS + 2) * BLOCK))
    for m in range(PRODUCTS):
        part = decay_terms(t - CENTRE if m < 3 else CENTRE - t, SHORT_TERMS).T
        rows = slice(m * SHORT_TERMS, (m + 1) * SHORT_TERMS)
        moments[rows, m * BLOCK : (m + 1) * BLOCK] = part
    moments[LAG_ROW : LAG_ROW + TERMS, PRODUCTS * BLOCK :] = ahead.T @ back
    blank = np.zeros((16 - TERMS, BLOCK))
    taps = np.zeros((16, TERMS))
    taps[:3] = decay_terms([-CENTRE, 1 - CENTRE, -1 - CENTRE])
    edge = np.zeros((16, TERMS))
    edge[:2] = decay_terms([-CENTRE, -1 - CENTRE])

    def padded(table, repeat=0):
        out = np.zeros((table.shape[0], 16))
        out[:, :TERMS] = table
        out[:, TERMS : TERMS + repeat] = table[:, :repeat]
        return out

    first, second = decay_terms([-CENTRE, 1 - CENTRE])

    def tripled(table):
        high, low = halves(padded(table))
        return np.concatenate([high, high, low], axis=1)

    carried = np.zeros((2 * BLOCK + 16, 64))
    carried[:BLOCK, :32] = paired(padded(ahead, 16 - TERMS))
    carried[BLOCK : 2 * BLOCK, 32:] = paired(padded(behind, 16 - TERMS))
    carried[2 * BLOCK :, 32:] = paired(padded(edge, 16 - TERMS))
    return dict(
        moments=moments.astype(BF16),
        fore_u=paired(np.concatenate([fore, behind.T, blank], axis=0)),
        fore_g=paired(np.concatenate([fore, ahead.T, blank], axis=0)),
        impulse=tripled(np.concatenate([fore @ ahead, taps], axis=0)),
        back=back.astype(BF16),
        carried=carried.astype(BF16),
        first=[float(x) for x in first],
        second=[float(x) for x in second],
    )


def dot(left, right):
    return jnp.dot(left, right, preferred_element_type=F32)


def whole(shape):
    return pl.BlockSpec(shape, lambda *_: (0,) * len(shape))


def later_rows(values, before, by):
    moved = pltpu.roll(values, by, 0)
    top = moved[:8]
    row = lax.broadcasted_iota(jnp.int32, top.shape, 0)
    for i in range(by):
        top = jnp.where(row == i, before[2 - by + i : 3 - by + i], top)
    return jnp.concatenate([top, moved[8:]], axis=0)


def sooner_rows(values, after):
    count = values.shape[0]
    moved = pltpu.roll(values, count - 1, 0)
    row = lax.broadcasted_iota(jnp.int32, (8, values.shape[1]), 0)
    bottom = jnp.where(row == 7, after, moved[count - 8 :])
    return jnp.concatenate([moved[: count - 8], bottom], axis=0)


def lanes_of(ref, rows, chunks):
    return jnp.concatenate([ref[i, rows, :] for i in range(chunks.start, chunks.stop)], axis=1)


def store_chunks(ref, chunks, start, rows):
    rows = rows.astype(BF16)
    for i in range(chunks.stop - chunks.start):
        ref[chunks.start + i, start : start + rows.shape[0], :] = rows[:, i * LANES : (i + 1) * LANES]


def edge_rows(skip, refs):
    rows = [ref[0].astype(F32)[skip : skip + 2] for ref in refs]
    rows.extend([jnp.zeros_like(rows[0])] * (4 - len(rows)))
    return jnp.concatenate(rows, axis=0).astype(BF16)


def front_kernel(*refs):
    refs[-1][...] = edge_rows(0, refs[:-1])


def prep_kernel(
    amount_ref, rate_ref, query_ref, key_ref, value_ref,
    root_ref, basis_ref, slope_ref, loaded_ref, spread_ref, last_ref,
):
    last_ref[...] = edge_rows(14, (query_ref, key_ref, value_ref))
    amount, rate = amount_ref[...], rate_ref[...]
    square = rate * rate
    sinh = rate * (1.0 + square * (1.0 / 6.0 + square * (1.0 / 120.0)))
    root = jnp.sqrt(2.0 * jnp.exp(-rate) * sinh)
    root_ref[...] = root
    weight = amount * root
    centred = weight * jnp.exp(-float(CENTRE) * rate)
    spot = rate * (2.0 / TOP_RATE) - 1.0
    value, older = jnp.ones_like(spot), spot
    slope, older_slope = jnp.zeros_like(spot), jnp.zeros_like(spot)
    rows = []
    for k in range(TERMS):
        basis_ref[k] = value
        slope_ref[k] = slope * (-2.0 / TOP_RATE)
        loaded_ref[k] = value * weight
        rows.append(jnp.sum(value * centred, axis=0, keepdims=True))
        if k == 0:
            following, following_slope = spot, jnp.ones_like(spot)
        else:
            following = 2.0 * spot * value - older
            following_slope = 2.0 * value + 2.0 * spot * slope - older_slope
        older, older_slope = value, slope
        value, slope = following, following_slope
    rows.append(jnp.zeros((16 - TERMS, LANES), F32))
    coefs = jnp.concatenate(rows, axis=0)
    high = coefs.astype(BF16)
    low = (coefs - high.astype(F32)).astype(BF16)
    both = jnp.concatenate([high, low], axis=0)
    spread_ref[...] = jnp.broadcast_to(both[None], spread_ref.shape)


def interleave(waiting, skew):
    active, turn = [], 0
    while waiting or active:
        if waiting and turn % skew == 0:
            active.append(waiting.pop(0))
        for steps in list(active):
            if next(steps, active) is active:
                active.remove(steps)
        turn += 1


def block_kernel(
    query_ref, key_ref, value_ref, cot_ref, filter_ref, before_ref, coefs_ref,
    fore_u_ref, fore_g_ref, impulse_ref, back_ref, moments_ref,
    sent_ref, mixed_ref, grad_ref, key_short_ref, value_short_ref, impulse_out, products,
):
    width = mixed_ref.shape[1]
    step = min(INNER, width)
    waiting = [
        block_columns(
            slice(start, start + step), slice(start // LANES, (start + step) // LANES),
            query_ref, key_ref, value_ref, cot_ref, filter_ref, before_ref, coefs_ref,
            fore_u_ref, fore_g_ref, impulse_ref, back_ref, moments_ref,
            sent_ref, mixed_ref, grad_ref, key_short_ref, value_short_ref, impulse_out, products,
        )
        for start in range(0, width, step)
    ]
    interleave(waiting, SKEW)


def block_columns(
    at, chunks,
    query_ref, key_ref, value_ref, cot_ref, filter_ref, before_ref, coefs_ref,
    fore_u_ref, fore_g_ref, impulse_ref, back_ref, moments_ref,
    sent_ref, mixed_ref, grad_ref, key_short_ref, value_short_ref, impulse_out, products,
):
    before = before_ref[:, at].astype(F32)
    query, key, value = (ref[0, :, at].astype(F32) for ref in (query_ref, key_ref, value_ref))
    cot = cot_ref[0, :, at].astype(F32)

    def lagged(i, x):
        edge = before[2 * i : 2 * i + 2]
        return (x, later_rows(x, edge, 1), later_rows(x, edge, 2))

    def short(i, inputs):
        return sum(filter_ref[i, j : j + 1, at] * inputs[j] for j in range(3))

    queries, keys, values = lagged(0, query), lagged(1, key), lagged(2, value)
    key_short, value_short = short(1, keys), short(2, values)
    key_short_ref[:, at] = key_short.astype(BF16)
    value_short_ref[:, at] = value_short.astype(BF16)
    gated = (key_short * value_short).astype(BF16)
    grad_mixed = (cot * short(0, queries)).astype(BF16)
    for i, (left, inputs) in enumerate(((cot, queries), (value_short, keys), (key_short, values))):
        for j in range(3):
            start = (3 * i + j) * BLOCK
            products[start : start + BLOCK, at] = (left * inputs[j]).astype(BF16)

    yield
    u = dot(fore_u_ref[...], jnp.concatenate([gated, gated], axis=0))
    g = dot(fore_g_ref[...], jnp.concatenate([grad_mixed, grad_mixed], axis=0))
    coefs = lanes_of(coefs_ref, slice(None), chunks)
    h = dot(impulse_ref[...], jnp.concatenate([coefs, coefs[:16]], axis=0))
    impulse_out[:, at] = h[2 * FREQS : 2 * FREQS + 8]
    yield
    ur, ui, gr, gi, hr, hi = (
        x[part * FREQS : (part + 1) * FREQS] for x in (u, g, h) for part in (0, 1)
    )

    def spectrum(real, imag):
        return jnp.concatenate([real.astype(BF16), imag.astype(BF16)], axis=0)

    products[PRODUCTS * BLOCK :, at] = spectrum(gr * ur + gi * ui, gi * ur - gr * ui)
    mixed = dot(back_ref[...], spectrum(ur * hr - ui * hi, ur * hi + ui * hr))
    grad = dot(back_ref[...], spectrum(gr * hr + gi * hi, gi * hr - gr * hi))
    yield
    mixed_ref[:, at] = mixed.astype(BF16)
    grad_ref[:, at] = grad.astype(BF16)
    row = lax.broadcasted_iota(jnp.int32, (16, mixed.shape[1]), 0)
    sums = [u[2 * FREQS :], g[2 * FREQS :]]
    spare = 16 - TERMS
    for i, (inputs, weight) in enumerate(
        ((queries, cot * mixed), (keys, value_short * grad), (values, key_short * grad))
    ):
        for j in range(3):
            m = 3 * i + j
            local = jnp.sum(inputs[j] * weight, axis=0, keepdims=True)
            sums[m // spare] = jnp.where(row == TERMS + m % spare, local, sums[m // spare])
    yield
    store_chunks(sent_ref, chunks, 0, dot(moments_ref[...], products[:, at]))
    store_chunks(sent_ref, chunks, SUM_ROW, sums[0])
    store_chunks(sent_ref, chunks, SUM_ROW + 16, sums[1])


def owner_kernel(
    first, second, moments_ref, basis_ref, slope_ref, loaded_ref, rate_ref, root_ref, amount_ref,
    carry_ref, message_ref, ahead, behind,
):
    blocks = moments_ref.shape[1]
    modes = rate_ref.shape[0]
    row = lax.broadcasted_iota(jnp.int32, (blocks, LANES), 0)
    lag, sum_u, sum_g, spare = LAG_ROW, SUM_ROW, SUM_ROW + 16, 16 - TERMS

    def later(x, by):
        return jnp.where(row >= by, pltpu.roll(x, by, 0), 0.0)

    def sooner(x, by):
        return jnp.where(row < blocks - by, pltpu.roll(x, blocks - by, 0), 0.0)

    lag_rows = [jnp.sum(moments_ref[lag + k], axis=0, keepdims=True) for k in range(TERMS)]
    first_rows, second_rows = [], []
    for n in range(modes):
        basis = [basis_ref[k, n : n + 1, :] for k in range(TERMS)]
        slope = [slope_ref[k, n : n + 1, :] for k in range(TERMS)]
        state = sum(basis[k] * moments_ref[sum_u + k] for k in range(TERMS))
        state_slope = sum(slope[k] * moments_ref[sum_u + k] for k in range(1, TERMS))
        grad = sum(basis[k] * moments_ref[sum_g + k] for k in range(TERMS))
        grad_slope = sum(slope[k] * moments_ref[sum_g + k] for k in range(1, TERMS))
        rate = rate_ref[n : n + 1, :]
        half = jnp.exp(-float(CENTRE) * rate)
        factor = half * half
        moved = later(state, 1)
        forward = factor * moved
        forward_slope = factor * (later(state_slope, 1) + float(BLOCK) * moved)
        backward = factor * sooner(grad, 1)
        by = 1
        while by < blocks:
            moved = later(forward, by)
            forward_slope = forward_slope + factor * (
                later(forward_slope, by) + float(BLOCK * by) * moved
            )
            forward = forward + factor * moved
            backward = backward + factor * sooner(backward, by)
            factor = factor * factor
            by *= 2
        ahead[n] = forward
        behind[n] = backward
        first_sum = jnp.sum(forward * grad, axis=0, keepdims=True)
        second_sum = jnp.sum(forward_slope * grad + forward * grad_slope, axis=0, keepdims=True)
        near = half * sum(basis[k] * lag_rows[k] for k in range(TERMS))
        near_slope = half * sum(slope[k] * lag_rows[k] for k in range(1, TERMS))
        first_rows.append(first_sum + near)
        second_rows.append(second_sum + near_slope + float(CENTRE) * near)
    totals = [moments_ref[SUM_ROW + 16 * (m // spare) + TERMS + m % spare] for m in range(PRODUCTS)]
    edge_one, edge_two = 0.0, 0.0
    for k in range(TERMS):
        carry = sum(loaded_ref[k, n : n + 1, :] * ahead[n] for n in range(modes))
        back = sum(loaded_ref[k, n : n + 1, :] * behind[n] for n in range(modes))
        for start, value in ((0, carry), (16, back)):
            high = value.astype(BF16)
            carry_ref[start + k] = high
            if k < 16 - TERMS:
                carry_ref[start + TERMS + k] = (value - high.astype(F32)).astype(BF16)
        edge_one = edge_one + first[k] * carry
        edge_two = edge_two + second[k] * carry
        if k < SHORT_TERMS:
            for m in range(PRODUCTS):
                totals[m] = totals[m] + (carry if m < 3 else back) * moments_ref[m * SHORT_TERMS + k]
    carry_ref[32] = sooner(edge_one, 1).astype(BF16)
    carry_ref[33] = sooner(edge_two, 1).astype(BF16)
    root, amount = root_ref[...], amount_ref[...]
    first_sum = jnp.concatenate(first_rows, axis=0)
    second_sum = jnp.concatenate(second_rows, axis=0)
    rate = rate_ref[...]
    steep = amount * (jnp.exp(-2.0 * rate) / root * first_sum - root * second_sum)
    for i in range(34, CARRY_ROWS):
        carry_ref[i] = jnp.zeros((blocks, LANES), BF16)
    rows = [jnp.zeros((2, LANES), F32)]
    rows.extend(jnp.sum(total, axis=0, keepdims=True) for total in totals)
    rows.append(jnp.zeros((14 - PRODUCTS, LANES), F32))
    message = jnp.concatenate([*rows, root * first_sum, rate * steep], axis=0).astype(BF16)
    message_ref[...] = jnp.broadcast_to(message[None], message_ref.shape)


def total_kernel(factor, message_ref, carry_ref, sent_ref, residue_ref, decay_ref):
    total = message_ref[0].astype(F32)
    for i in range(1, message_ref.shape[0]):
        total = total + message_ref[i].astype(F32)
    total = total * factor
    modes = residue_ref.shape[0]
    residue_ref[...] = total[16 : 16 + modes]
    decay_ref[...] = total[16 + modes :]
    shared = total[:16]
    for block in range(sent_ref.shape[0]):
        sent_ref[block, :32, :] = carry_ref[block, :32, :]
        sent_ref[block, 32:48, :] = (carry_ref[block, 32:48, :].astype(F32) + shared).astype(BF16)


def edge_kernel(query_end, key_end, value_end, filter_ref, after_ref, impulse_ref, edge_ref):
    after, impulse = after_ref[...].astype(F32), impulse_ref[...]

    def rounded(x):
        return x.astype(BF16).astype(F32)

    def short_after(i, ref):
        last, following = ref[0].astype(F32)[14:], after[2 * i : 2 * i + 2]
        middle = jnp.concatenate([last[1:2], following[0:1]], axis=0)
        zero, one, two = (filter_ref[i, j : j + 1, :] for j in range(3))
        return zero * following + one * middle + two * last

    query_next, key_next, value_next = (
        short_after(i, ref) for i, ref in enumerate((query_end, key_end, value_end))
    )
    gated_next = rounded(key_next * value_next)
    grad_mixed_next = rounded(after[6:7] * query_next[0:1])
    edge_ref[...] = jnp.concatenate(
        [
            impulse[0:1] * gated_next[0:1],
            impulse[0:1] * gated_next[1:2] + impulse[1:2] * gated_next[0:1],
            -impulse[2:3] * grad_mixed_next,
            jnp.zeros_like(grad_mixed_next),
            key_next,
            value_next,
        ],
        axis=0,
    )


def finish_kernel(
    cot_ref, filter_ref, after_ref, local_edge_ref, key_short_ref, value_short_ref,
    mixed_ref, grad_ref, carry_ref, carried_ref,
    query_out, key_out, value_out, filter_out,
):
    step = min(INNER, mixed_ref.shape[1])
    for start in range(0, mixed_ref.shape[1], step):
        finish_columns(
            slice(start, start + step), slice(start // LANES, (start + step) // LANES),
            cot_ref, filter_ref, after_ref, local_edge_ref, key_short_ref, value_short_ref,
            mixed_ref, grad_ref, carry_ref, carried_ref,
            query_out, key_out, value_out, filter_out,
        )


def finish_columns(
    at, chunks,
    cot_ref, filter_ref, after_ref, local_edge_ref, key_short_ref, value_short_ref,
    mixed_ref, grad_ref, carry_ref, carried_ref,
    query_out, key_out, value_out, filter_out,
):
    after, local_edge = after_ref[:, at].astype(F32), local_edge_ref[:, at]

    def tap(i, j):
        return filter_ref[i, j : j + 1, at]

    both = lanes_of(carry_ref, slice(0, 32), chunks)
    both = jnp.concatenate([both[:16], both[:16], both[16:], both[16:]], axis=0)
    carried = dot(carried_ref[...], both)
    rest = lanes_of(carry_ref, slice(32, 48), chunks).astype(F32)
    for m in range(PRODUCTS):
        filter_out[m // 3, m % 3 : m % 3 + 1, at] = rest[2 + m : 3 + m]
    mixed = mixed_ref[:, at].astype(F32) + carried[:BLOCK]
    grad = grad_ref[:, at].astype(F32) + carried[BLOCK : 2 * BLOCK]
    edge = carried[2 * BLOCK :]
    mixed_next = rest[0:1] + local_edge[0:1], rest[1:2] + local_edge[1:2]
    grad_next = edge[0:1], edge[1:2] + local_edge[2:3]

    cot = cot_ref[0, :, at].astype(F32)
    for i, (out_ref, left, right, left_next, right_next) in enumerate(
        (
            (query_out, cot, mixed, after[6:8], mixed_next),
            (key_out, value_short_ref[:, at].astype(F32), grad, local_edge[6:8], grad_next),
            (value_out, key_short_ref[:, at].astype(F32), grad, local_edge[4:6], grad_next),
        )
    ):
        zero, one, two = (tap(i, j) for j in range(3))
        here = left * right
        following = left_next[0:1] * right_next[0]
        inner = one * here + sooner_rows(two * here, two * following)
        inner_after = one * following + two * (left_next[1:2] * right_next[1])
        out_ref[0, :, at] = (zero * here + sooner_rows(inner, inner_after)).astype(BF16)


def body(query_rows, key_rows, value_rows, cotangent, short_filter, residue, decay_rate):
    width = query_rows.shape[2]
    blocks = lax.axis_size("seq")
    groups = lax.axis_size("dp")
    modes = residue.shape[1]
    length = BLOCK * blocks
    wide = min(WIDE, width)
    parts = wide // LANES
    grid = (width // wide,)
    tables = make_tables()
    first, second = tables.pop("first"), tables.pop("second")
    tables = {name: jnp.asarray(table) for name, table in tables.items()}
    params = pltpu.CompilerParams(vmem_limit_bytes=VMEM_LIMIT)
    full_params = pltpu.CompilerParams(vmem_limit_bytes=FULL_LIMIT)
    small_params = pltpu.CompilerParams(vmem_limit_bytes=SMALL_LIMIT)

    def shape(*dims, dtype=F32):
        return jax.ShapeDtypeStruct(dims, dtype)

    def edge_spec(end):
        return pl.BlockSpec((1, 16, width), lambda c: (0, (BLOCK // 16 - 1) * end, 0))

    flip, small = shape(modes, LANES), shape(TERMS, modes, LANES)
    amount_t, rate_t = residue.T, decay_rate.T
    edges = shape(8, width, dtype=BF16)
    outs = (flip, small, small, small, shape(blocks, 32, LANES, dtype=BF16), edges)
    root_t, basis, slope, loaded, spread, last = pl.pallas_call(
        prep_kernel,
        grid=(1,),
        in_specs=[whole(flip.shape)] * 2 + [edge_spec(1)] * 3,
        out_specs=[whole(out.shape) for out in outs],
        out_shape=outs,
        compiler_params=params,
        name="prep",
    )(amount_t, rate_t, query_rows, key_rows, value_rows)
    before = lax.ppermute(last, "seq", [(i, i + 1) for i in range(blocks - 1)])
    coefs = lax.all_to_all(spread, "seq", 0, 0, tiled=True)

    tall = pl.BlockSpec((1, BLOCK, wide), lambda c: (0, 0, c))
    filters = pl.BlockSpec((3, 3, wide), lambda c: (0, 0, c))

    def flat(rows):
        return pl.BlockSpec((rows, wide), lambda c: (0, c))

    def chunks(rows):
        return pl.BlockSpec((parts, rows, LANES), lambda c: (c, 0, 0))

    def table_specs(names):
        return [whole(tables[name].shape) for name in names]

    names = ("fore_u", "fore_g", "impulse", "back", "moments")
    half = shape(BLOCK, width, dtype=BF16)
    sent, mixed, grad, key_short, value_short, impulse = pl.pallas_call(
        block_kernel,
        grid=grid,
        in_specs=[tall] * 4 + [filters, flat(8), chunks(32)] + table_specs(names),
        out_specs=(chunks(SENT_ROWS), *[flat(BLOCK)] * 4, flat(8)),
        out_shape=(shape(blocks, SENT_ROWS, LANES, dtype=BF16), half, half, half, half, shape(8, width)),
        scratch_shapes=[pltpu.VMEM(((PRODUCTS + 2) * BLOCK, wide), BF16)],
        compiler_params=full_params,
        name="block",
    )(
        query_rows, key_rows, value_rows, cotangent, short_filter, before, coefs,
        *[tables[name] for name in names],
    )
    front = pl.pallas_call(
        front_kernel,
        grid=(1,),
        in_specs=[edge_spec(0)] * 4,
        out_specs=whole((8, width)),
        out_shape=edges,
        compiler_params=params,
        name="front",
    )(query_rows, key_rows, value_rows, cotangent)
    sent, front = lax.optimization_barrier((sent, front))
    moments = lax.all_to_all(sent, "seq", 0, 0, tiled=True)
    after = lax.ppermute(front, "seq", [(i + 1, i) for i in range(blocks - 1)])
    moments, after = lax.optimization_barrier((moments, after))
    moments = moments.transpose(1, 0, 2).astype(F32)

    carry, message = pl.pallas_call(
        lambda *refs: owner_kernel(first, second, *refs),
        out_shape=(
            shape(CARRY_ROWS, blocks, LANES, dtype=BF16),
            shape(groups, 16 + 2 * modes, LANES, dtype=BF16),
        ),
        scratch_shapes=[pltpu.VMEM((modes, blocks, LANES), F32)] * 2,
        compiler_params=small_params,
        name="owner",
    )(moments, basis, slope, loaded, rate_t, root_t, amount_t)
    message = lax.all_to_all(message, "dp", 0, 0, tiled=True)
    local_edge = pl.pallas_call(
        edge_kernel,
        grid=(1,),
        in_specs=[edge_spec(1)] * 3 + [whole((3, 3, width)), whole((8, width)), whole((8, width))],
        out_specs=whole((8, width)),
        out_shape=shape(8, width),
        compiler_params=params,
        name="edge",
    )(query_rows, key_rows, value_rows, short_filter, after, impulse)
    message, local_edge = lax.optimization_barrier((message, local_edge))
    factor = 1.0 / math.sqrt(query_rows.shape[0] * groups * length)
    sent, residue_grad, decay_grad = pl.pallas_call(
        lambda *refs: total_kernel(factor, *refs),
        out_shape=(shape(blocks, CARRY_ROWS, LANES, dtype=BF16), flip, flip),
        compiler_params=small_params,
        name="total",
    )(message, carry.transpose(1, 0, 2))
    carry = lax.all_to_all(sent, "seq", 0, 0, tiled=True)

    names = ("carried",)
    *outs, filter_grad = pl.pallas_call(
        finish_kernel,
        grid=grid,
        in_specs=[tall, filters, flat(8), flat(8)] + [flat(BLOCK)] * 4
        + [chunks(CARRY_ROWS)] + table_specs(names),
        out_specs=[tall] * 3 + [filters],
        out_shape=[jax.ShapeDtypeStruct(query_rows.shape, BF16)] * 3 + [shape(3, 3, width)],
        compiler_params=params,
        name="finish",
    )(
        cotangent, short_filter, after, local_edge, key_short, value_short,
        mixed, grad, carry, *[tables[name] for name in names],
    )
    return (*outs, filter_grad, residue_grad.T, decay_grad.T)


def solution(mesh):
    rows = P("dp", "seq", None)
    return jax.shard_map(
        body,
        mesh=mesh,
        in_specs=(rows, rows, rows, rows, P(), P("seq", None), P("seq", None)),
        out_specs=(rows, rows, rows, P(), P("seq", None), P("seq", None)),
        check_vma=False,
    )
```

```python
import math

import jax
import jax.numpy as jnp
import numpy as np
from jax import lax
from jax.experimental import pallas as pl
from jax.experimental.pallas import tpu as pltpu
from jax.sharding import PartitionSpec as P

BLOCK = 128
CENTRE = BLOCK // 2
TERMS = 10
SHORT_TERMS = 9
PRODUCTS = 9
SENT_ROWS = 128
LAG_ROW = PRODUCTS * SHORT_TERMS
SUM_ROW = 96
CARRY_ROWS = 48
TOP_RATE = 1.0 / 32.0
FREQS = 128
LANES = 128
BF16 = jnp.bfloat16
F32 = jnp.float32
VMEM_LIMIT = 63 * 1024 * 1024
FULL_LIMIT = 64 * 1024 * 1024 - 65536
SMALL_LIMIT = 16 * 1024 * 1024
WIDE = 1024
INNER = 256
SKEW = 2
ORDERED = False


def decay_terms(times, terms=TERMS):
    points = 64
    theta = (np.arange(points) + 0.5) * np.pi / points
    rates = (np.cos(theta) + 1.0) * TOP_RATE / 2.0
    values = np.exp(-np.asarray(times, np.float64)[:, None] * rates[None, :])
    basis = np.cos(np.arange(terms)[None, :] * theta[:, None]) * (2.0 / points)
    basis[:, 0] *= 0.5
    return values @ basis


def halves(table):
    table = np.asarray(table, np.float32)
    high = table.astype(BF16)
    low = (table - high.astype(np.float32)).astype(BF16)
    return high, low


def paired(table):
    return np.concatenate(halves(table), axis=1)


def make_tables():
    t = np.arange(BLOCK)
    angle = 2.0 * np.pi / (2 * FREQS) * (np.arange(FREQS)[:, None] + 0.5) * t[None, :]
    fore = np.concatenate([np.cos(angle), -np.sin(angle)], axis=0)
    back = np.concatenate([np.cos(angle.T), -np.sin(angle.T)], axis=1) / FREQS
    ahead = decay_terms(t - CENTRE)
    behind = decay_terms(CENTRE - t)
    moments = np.zeros((SUM_ROW, (PRODUCTS + 2) * BLOCK))
    for m in range(PRODUCTS):
        part = decay_terms(t - CENTRE if m < 3 else CENTRE - t, SHORT_TERMS).T
        rows = slice(m * SHORT_TERMS, (m + 1) * SHORT_TERMS)
        moments[rows, m * BLOCK : (m + 1) * BLOCK] = part
    moments[LAG_ROW : LAG_ROW + TERMS, PRODUCTS * BLOCK :] = ahead.T @ back
    blank = np.zeros((16 - TERMS, BLOCK))
    taps = np.zeros((16, TERMS))
    taps[:3] = decay_terms([-CENTRE, 1 - CENTRE, -1 - CENTRE])
    edge = np.zeros((16, TERMS))
    edge[:2] = decay_terms([-CENTRE, -1 - CENTRE])

    def padded(table, repeat=0):
        out = np.zeros((table.shape[0], 16))
        out[:, :TERMS] = table
        out[:, TERMS : TERMS + repeat] = table[:, :repeat]
        return out

    first, second = decay_terms([-CENTRE, 1 - CENTRE])

    def tripled(table):
        high, low = halves(padded(table))
        return np.concatenate([high, high, low], axis=1)

    carried = np.zeros((2 * BLOCK + 16, 64))
    carried[:BLOCK, :32] = paired(padded(ahead, 16 - TERMS))
    carried[BLOCK : 2 * BLOCK, 32:] = paired(padded(behind, 16 - TERMS))
    carried[2 * BLOCK :, 32:] = paired(padded(edge, 16 - TERMS))
    return dict(
        moments=moments.astype(BF16),
        fore_u=paired(np.concatenate([fore, behind.T, blank], axis=0)),
        fore_g=paired(np.concatenate([fore, ahead.T, blank], axis=0)),
        impulse=tripled(np.concatenate([fore @ ahead, taps], axis=0)),
        back=back.astype(BF16),
        carried=carried.astype(BF16),
        first=[float(x) for x in first],
        second=[float(x) for x in second],
    )


def dot(left, right):
    return jnp.dot(left, right, preferred_element_type=F32)


def whole(shape):
    return pl.BlockSpec(shape, lambda *_: (0,) * len(shape))


def later_rows(values, before, by):
    moved = pltpu.roll(values, by, 0)
    top = moved[:8]
    row = lax.broadcasted_iota(jnp.int32, top.shape, 0)
    for i in range(by):
        top = jnp.where(row == i, before[2 - by + i : 3 - by + i], top)
    return jnp.concatenate([top, moved[8:]], axis=0)


def sooner_rows(values, after):
    count = values.shape[0]
    moved = pltpu.roll(values, count - 1, 0)
    row = lax.broadcasted_iota(jnp.int32, (8, values.shape[1]), 0)
    bottom = jnp.where(row == 7, after, moved[count - 8 :])
    return jnp.concatenate([moved[: count - 8], bottom], axis=0)


def lanes_of(ref, rows, chunks):
    return jnp.concatenate([ref[i, rows, :] for i in range(chunks.start, chunks.stop)], axis=1)


def store_chunks(ref, chunks, start, rows):
    rows = rows.astype(BF16)
    for i in range(chunks.stop - chunks.start):
        ref[chunks.start + i, start : start + rows.shape[0], :] = rows[:, i * LANES : (i + 1) * LANES]


def edge_rows(skip, refs):
    rows = [ref[0].astype(F32)[skip : skip + 2] for ref in refs]
    rows.extend([jnp.zeros_like(rows[0])] * (4 - len(rows)))
    return jnp.concatenate(rows, axis=0).astype(BF16)


def front_kernel(*refs):
    refs[-1][...] = edge_rows(0, refs[:-1])


def prep_kernel(
    amount_ref, rate_ref, query_ref, key_ref, value_ref,
    root_ref, basis_ref, slope_ref, loaded_ref, spread_ref, last_ref,
):
    last_ref[...] = edge_rows(14, (query_ref, key_ref, value_ref))
    amount, rate = amount_ref[...], rate_ref[...]
    square = rate * rate
    sinh = rate * (1.0 + square * (1.0 / 6.0 + square * (1.0 / 120.0)))
    root = jnp.sqrt(2.0 * jnp.exp(-rate) * sinh)
    root_ref[...] = root
    weight = amount * root
    centred = weight * jnp.exp(-float(CENTRE) * rate)
    spot = rate * (2.0 / TOP_RATE) - 1.0
    value, older = jnp.ones_like(spot), spot
    slope, older_slope = jnp.zeros_like(spot), jnp.zeros_like(spot)
    rows = []
    for k in range(TERMS):
        basis_ref[k] = value
        slope_ref[k] = slope * (-2.0 / TOP_RATE)
        loaded_ref[k] = value * weight
        rows.append(jnp.sum(value * centred, axis=0, keepdims=True))
        if k == 0:
            following, following_slope = spot, jnp.ones_like(spot)
        else:
            following = 2.0 * spot * value - older
            following_slope = 2.0 * value + 2.0 * spot * slope - older_slope
        older, older_slope = value, slope
        value, slope = following, following_slope
    rows.append(jnp.zeros((16 - TERMS, LANES), F32))
    coefs = jnp.concatenate(rows, axis=0)
    high = coefs.astype(BF16)
    low = (coefs - high.astype(F32)).astype(BF16)
    both = jnp.concatenate([high, low], axis=0)
    spread_ref[...] = jnp.broadcast_to(both[None], spread_ref.shape)


def interleave(waiting, skew):
    active, turn = [], 0
    while waiting or active:
        if waiting and turn % skew == 0:
            active.append(waiting.pop(0))
        for steps in list(active):
            if next(steps, active) is active:
                active.remove(steps)
        turn += 1


def block_kernel(
    query_ref, key_ref, value_ref, cot_ref, filter_ref, before_ref, coefs_ref,
    fore_u_ref, fore_g_ref, impulse_ref, back_ref, moments_ref,
    sent_ref, mixed_ref, grad_ref, key_short_ref, value_short_ref, impulse_out, products,
):
    width = mixed_ref.shape[1]
    step = min(INNER, width)
    waiting = [
        block_columns(
            slice(start, start + step), slice(start // LANES, (start + step) // LANES),
            query_ref, key_ref, value_ref, cot_ref, filter_ref, before_ref, coefs_ref,
            fore_u_ref, fore_g_ref, impulse_ref, back_ref, moments_ref,
            sent_ref, mixed_ref, grad_ref, key_short_ref, value_short_ref, impulse_out, products,
        )
        for start in range(0, width, step)
    ]
    interleave(waiting, SKEW)


def block_columns(
    at, chunks,
    query_ref, key_ref, value_ref, cot_ref, filter_ref, before_ref, coefs_ref,
    fore_u_ref, fore_g_ref, impulse_ref, back_ref, moments_ref,
    sent_ref, mixed_ref, grad_ref, key_short_ref, value_short_ref, impulse_out, products,
):
    before = before_ref[:, at].astype(F32)
    query, key, value = (ref[0, :, at].astype(F32) for ref in (query_ref, key_ref, value_ref))
    cot = cot_ref[0, :, at].astype(F32)

    def lagged(i, x):
        edge = before[2 * i : 2 * i + 2]
        return (x, later_rows(x, edge, 1), later_rows(x, edge, 2))

    def short(i, inputs):
        return sum(filter_ref[i, j : j + 1, at] * inputs[j] for j in range(3))

    queries, keys, values = lagged(0, query), lagged(1, key), lagged(2, value)
    key_short, value_short = short(1, keys), short(2, values)
    key_short_ref[:, at] = key_short.astype(BF16)
    value_short_ref[:, at] = value_short.astype(BF16)
    gated = (key_short * value_short).astype(BF16)
    grad_mixed = (cot * short(0, queries)).astype(BF16)
    for i, (left, inputs) in enumerate(((cot, queries), (value_short, keys), (key_short, values))):
        for j in range(3):
            start = (3 * i + j) * BLOCK
            products[start : start + BLOCK, at] = left.astype(BF16) * inputs[j].astype(BF16)

    yield
    u = dot(fore_u_ref[...], jnp.concatenate([gated, gated], axis=0))
    g = dot(fore_g_ref[...], jnp.concatenate([grad_mixed, grad_mixed], axis=0))
    coefs = lanes_of(coefs_ref, slice(None), chunks)
    h = dot(impulse_ref[...], jnp.concatenate([coefs, coefs[:16]], axis=0))
    impulse_out[:, at] = h[2 * FREQS : 2 * FREQS + 8]
    yield
    ur, ui, gr, gi, hr, hi = (
        x[part * FREQS : (part + 1) * FREQS].astype(BF16) for x in (u, g, h) for part in (0, 1)
    )

    def spectrum(real, imag):
        return jnp.concatenate([real.astype(BF16), imag.astype(BF16)], axis=0)

    products[PRODUCTS * BLOCK :, at] = spectrum(gr * ur + gi * ui, gi * ur - gr * ui)
    mixed = dot(back_ref[...], spectrum(ur * hr - ui * hi, ur * hi + ui * hr))
    grad = dot(back_ref[...], spectrum(gr * hr + gi * hi, gi * hr - gr * hi))
    yield
    mixed_ref[:, at] = mixed.astype(BF16)
    grad_ref[:, at] = grad.astype(BF16)
    row = lax.broadcasted_iota(jnp.int32, (16, mixed.shape[1]), 0)
    sums = [u[2 * FREQS :], g[2 * FREQS :]]
    spare = 16 - TERMS
    for i, (inputs, weight) in enumerate(
        ((queries, cot * mixed), (keys, value_short * grad), (values, key_short * grad))
    ):
        for j in range(3):
            m = 3 * i + j
            local = jnp.sum(inputs[j] * weight, axis=0, keepdims=True)
            sums[m // spare] = jnp.where(row == TERMS + m % spare, local, sums[m // spare])
    yield
    store_chunks(sent_ref, chunks, 0, dot(moments_ref[...], products[:, at]))
    store_chunks(sent_ref, chunks, SUM_ROW, sums[0])
    store_chunks(sent_ref, chunks, SUM_ROW + 16, sums[1])


def owner_kernel(
    first, second, moments_ref, basis_ref, slope_ref, loaded_ref, rate_ref, root_ref, amount_ref,
    carry_ref, message_ref, ahead, behind,
):
    blocks = moments_ref.shape[1]
    modes = rate_ref.shape[0]
    row = lax.broadcasted_iota(jnp.int32, (blocks, LANES), 0)
    lag, sum_u, sum_g, spare = LAG_ROW, SUM_ROW, SUM_ROW + 16, 16 - TERMS

    def later(x, by):
        return jnp.where(row >= by, pltpu.roll(x, by, 0), 0.0)

    def sooner(x, by):
        return jnp.where(row < blocks - by, pltpu.roll(x, blocks - by, 0), 0.0)

    lag_rows = [jnp.sum(moments_ref[lag + k], axis=0, keepdims=True) for k in range(TERMS)]
    first_rows, second_rows = [], []
    for n in range(modes):
        basis = [basis_ref[k, n : n + 1, :] for k in range(TERMS)]
        slope = [slope_ref[k, n : n + 1, :] for k in range(TERMS)]
        state = sum(basis[k] * moments_ref[sum_u + k] for k in range(TERMS))
        state_slope = sum(slope[k] * moments_ref[sum_u + k] for k in range(1, TERMS))
        grad = sum(basis[k] * moments_ref[sum_g + k] for k in range(TERMS))
        grad_slope = sum(slope[k] * moments_ref[sum_g + k] for k in range(1, TERMS))
        rate = rate_ref[n : n + 1, :]
        half = jnp.exp(-float(CENTRE) * rate)
        factor = half * half
        moved = later(state, 1)
        forward = factor * moved
        forward_slope = factor * (later(state_slope, 1) + float(BLOCK) * moved)
        backward = factor * sooner(grad, 1)
        by = 1
        while by < blocks:
            moved = later(forward, by)
            forward_slope = forward_slope + factor * (
                later(forward_slope, by) + float(BLOCK * by) * moved
            )
            forward = forward + factor * moved
            backward = backward + factor * sooner(backward, by)
            factor = factor * factor
            by *= 2
        ahead[n] = forward
        behind[n] = backward
        first_sum = jnp.sum(forward * grad, axis=0, keepdims=True)
        second_sum = jnp.sum(forward_slope * grad + forward * grad_slope, axis=0, keepdims=True)
        near = half * sum(basis[k] * lag_rows[k] for k in range(TERMS))
        near_slope = half * sum(slope[k] * lag_rows[k] for k in range(1, TERMS))
        first_rows.append(first_sum + near)
        second_rows.append(second_sum + near_slope + float(CENTRE) * near)
    totals = [moments_ref[SUM_ROW + 16 * (m // spare) + TERMS + m % spare] for m in range(PRODUCTS)]
    edge_one, edge_two = 0.0, 0.0
    for k in range(TERMS):
        carry = sum(loaded_ref[k, n : n + 1, :] * ahead[n] for n in range(modes))
        back = sum(loaded_ref[k, n : n + 1, :] * behind[n] for n in range(modes))
        for start, value in ((0, carry), (16, back)):
            high = value.astype(BF16)
            carry_ref[start + k] = high
            if k < 16 - TERMS:
                carry_ref[start + TERMS + k] = (value - high.astype(F32)).astype(BF16)
        edge_one = edge_one + first[k] * carry
        edge_two = edge_two + second[k] * carry
        if k < SHORT_TERMS:
            for m in range(PRODUCTS):
                totals[m] = totals[m] + (carry if m < 3 else back) * moments_ref[m * SHORT_TERMS + k]
    carry_ref[32] = sooner(edge_one, 1).astype(BF16)
    carry_ref[33] = sooner(edge_two, 1).astype(BF16)
    root, amount = root_ref[...], amount_ref[...]
    first_sum = jnp.concatenate(first_rows, axis=0)
    second_sum = jnp.concatenate(second_rows, axis=0)
    rate = rate_ref[...]
    steep = amount * (jnp.exp(-2.0 * rate) / root * first_sum - root * second_sum)
    for i in range(34, CARRY_ROWS):
        carry_ref[i] = jnp.zeros((blocks, LANES), BF16)
    rows = [jnp.zeros((2, LANES), F32)]
    rows.extend(jnp.sum(total, axis=0, keepdims=True) for total in totals)
    rows.append(jnp.zeros((14 - PRODUCTS, LANES), F32))
    message = jnp.concatenate([*rows, root * first_sum, rate * steep], axis=0).astype(BF16)
    message_ref[...] = jnp.broadcast_to(message[None], message_ref.shape)


def total_kernel(factor, message_ref, carry_ref, sent_ref, residue_ref, decay_ref):
    total = message_ref[0].astype(F32)
    for i in range(1, message_ref.shape[0]):
        total = total + message_ref[i].astype(F32)
    total = total * factor
    modes = residue_ref.shape[0]
    residue_ref[...] = total[16 : 16 + modes]
    decay_ref[...] = total[16 + modes :]
    shared = total[:16]
    for block in range(sent_ref.shape[0]):
        sent_ref[block, :32, :] = carry_ref[block, :32, :]
        sent_ref[block, 32:48, :] = (carry_ref[block, 32:48, :].astype(F32) + shared).astype(BF16)


def edge_kernel(query_end, key_end, value_end, filter_ref, after_ref, impulse_ref, edge_ref):
    after, impulse = after_ref[...].astype(F32), impulse_ref[...]

    def rounded(x):
        return x.astype(BF16).astype(F32)

    def short_after(i, ref):
        last, following = ref[0].astype(F32)[14:], after[2 * i : 2 * i + 2]
        middle = jnp.concatenate([last[1:2], following[0:1]], axis=0)
        zero, one, two = (filter_ref[i, j : j + 1, :] for j in range(3))
        return zero * following + one * middle + two * last

    query_next, key_next, value_next = (
        short_after(i, ref) for i, ref in enumerate((query_end, key_end, value_end))
    )
    gated_next = rounded(key_next * value_next)
    grad_mixed_next = rounded(after[6:7] * query_next[0:1])
    edge_ref[...] = jnp.concatenate(
        [
            impulse[0:1] * gated_next[0:1],
            impulse[0:1] * gated_next[1:2] + impulse[1:2] * gated_next[0:1],
            -impulse[2:3] * grad_mixed_next,
            jnp.zeros_like(grad_mixed_next),
            key_next,
            value_next,
        ],
        axis=0,
    )


def finish_kernel(
    cot_ref, filter_ref, after_ref, local_edge_ref, key_short_ref, value_short_ref,
    mixed_ref, grad_ref, carry_ref, carried_ref,
    query_out, key_out, value_out, filter_out,
):
    step = min(INNER, mixed_ref.shape[1])
    for start in range(0, mixed_ref.shape[1], step):
        finish_columns(
            slice(start, start + step), slice(start // LANES, (start + step) // LANES),
            cot_ref, filter_ref, after_ref, local_edge_ref, key_short_ref, value_short_ref,
            mixed_ref, grad_ref, carry_ref, carried_ref,
            query_out, key_out, value_out, filter_out,
        )


def finish_columns(
    at, chunks,
    cot_ref, filter_ref, after_ref, local_edge_ref, key_short_ref, value_short_ref,
    mixed_ref, grad_ref, carry_ref, carried_ref,
    query_out, key_out, value_out, filter_out,
):
    after, local_edge = after_ref[:, at].astype(F32), local_edge_ref[:, at]

    def tap(i, j):
        return filter_ref[i, j : j + 1, at]

    both = lanes_of(carry_ref, slice(0, 32), chunks)
    both = jnp.concatenate([both[:16], both[:16], both[16:], both[16:]], axis=0)
    carried = dot(carried_ref[...], both)
    rest = lanes_of(carry_ref, slice(32, 48), chunks).astype(F32)
    for m in range(PRODUCTS):
        filter_out[m // 3, m % 3 : m % 3 + 1, at] = rest[2 + m : 3 + m]
    mixed = mixed_ref[:, at].astype(F32) + carried[:BLOCK]
    grad = grad_ref[:, at].astype(F32) + carried[BLOCK : 2 * BLOCK]
    edge = carried[2 * BLOCK :]
    mixed_next = rest[0:1] + local_edge[0:1], rest[1:2] + local_edge[1:2]
    grad_next = edge[0:1], edge[1:2] + local_edge[2:3]

    cot = cot_ref[0, :, at].astype(F32)
    for i, (out_ref, left, right, left_next, right_next) in enumerate(
        (
            (query_out, cot, mixed, after[6:8], mixed_next),
            (key_out, value_short_ref[:, at].astype(F32), grad, local_edge[6:8], grad_next),
            (value_out, key_short_ref[:, at].astype(F32), grad, local_edge[4:6], grad_next),
        )
    ):
        zero, one, two = (tap(i, j) for j in range(3))
        here = left * right
        following = left_next[0:1] * right_next[0]
        inner = one * here + sooner_rows(two * here, two * following)
        inner_after = one * following + two * (left_next[1:2] * right_next[1])
        out_ref[0, :, at] = (zero * here + sooner_rows(inner, inner_after)).astype(BF16)


def body(query_rows, key_rows, value_rows, cotangent, short_filter, residue, decay_rate):
    width = query_rows.shape[2]
    blocks = lax.axis_size("seq")
    groups = lax.axis_size("dp")
    modes = residue.shape[1]
    length = BLOCK * blocks
    wide = min(WIDE, width)
    parts = wide // LANES
    grid = (width // wide,)
    tables = make_tables()
    first, second = tables.pop("first"), tables.pop("second")
    tables = {name: jnp.asarray(table) for name, table in tables.items()}
    params = pltpu.CompilerParams(vmem_limit_bytes=VMEM_LIMIT)
    full_params = pltpu.CompilerParams(vmem_limit_bytes=FULL_LIMIT)
    small_params = pltpu.CompilerParams(vmem_limit_bytes=SMALL_LIMIT)

    def shape(*dims, dtype=F32):
        return jax.ShapeDtypeStruct(dims, dtype)

    def edge_spec(end):
        return pl.BlockSpec((1, 16, width), lambda c: (0, (BLOCK // 16 - 1) * end, 0))

    flip, small = shape(modes, LANES), shape(TERMS, modes, LANES)
    amount_t, rate_t = residue.T, decay_rate.T
    edges = shape(8, width, dtype=BF16)
    outs = (flip, small, small, small, shape(blocks, 32, LANES, dtype=BF16), edges)
    root_t, basis, slope, loaded, spread, last = pl.pallas_call(
        prep_kernel,
        grid=(1,),
        in_specs=[whole(flip.shape)] * 2 + [edge_spec(1)] * 3,
        out_specs=[whole(out.shape) for out in outs],
        out_shape=outs,
        compiler_params=params,
        name="prep",
    )(amount_t, rate_t, query_rows, key_rows, value_rows)
    before = lax.ppermute(last, "seq", [(i, i + 1) for i in range(blocks - 1)])
    coefs = lax.all_to_all(spread, "seq", 0, 0, tiled=True)

    tall = pl.BlockSpec((1, BLOCK, wide), lambda c: (0, 0, c))
    filters = pl.BlockSpec((3, 3, wide), lambda c: (0, 0, c))

    def flat(rows):
        return pl.BlockSpec((rows, wide), lambda c: (0, c))

    def chunks(rows):
        return pl.BlockSpec((parts, rows, LANES), lambda c: (c, 0, 0))

    def table_specs(names):
        return [whole(tables[name].shape) for name in names]

    names = ("fore_u", "fore_g", "impulse", "back", "moments")
    half = shape(BLOCK, width, dtype=BF16)
    sent, mixed, grad, key_short, value_short, impulse = pl.pallas_call(
        block_kernel,
        grid=grid,
        in_specs=[tall] * 4 + [filters, flat(8), chunks(32)] + table_specs(names),
        out_specs=(chunks(SENT_ROWS), *[flat(BLOCK)] * 4, flat(8)),
        out_shape=(shape(blocks, SENT_ROWS, LANES, dtype=BF16), half, half, half, half, shape(8, width)),
        scratch_shapes=[pltpu.VMEM(((PRODUCTS + 2) * BLOCK, wide), BF16)],
        compiler_params=full_params,
        name="block",
    )(
        query_rows, key_rows, value_rows, cotangent, short_filter, before, coefs,
        *[tables[name] for name in names],
    )
    front = pl.pallas_call(
        front_kernel,
        grid=(1,),
        in_specs=[edge_spec(0)] * 4,
        out_specs=whole((8, width)),
        out_shape=edges,
        compiler_params=params,
        name="front",
    )(query_rows, key_rows, value_rows, cotangent)
    sent, front = lax.optimization_barrier((sent, front))
    moments = lax.all_to_all(sent, "seq", 0, 0, tiled=True)
    after = lax.ppermute(front, "seq", [(i + 1, i) for i in range(blocks - 1)])
    moments, after = lax.optimization_barrier((moments, after))
    moments = moments.transpose(1, 0, 2).astype(F32)

    carry, message = pl.pallas_call(
        lambda *refs: owner_kernel(first, second, *refs),
        out_shape=(
            shape(CARRY_ROWS, blocks, LANES, dtype=BF16),
            shape(groups, 16 + 2 * modes, LANES, dtype=BF16),
        ),
        scratch_shapes=[pltpu.VMEM((modes, blocks, LANES), F32)] * 2,
        compiler_params=small_params,
        name="owner",
    )(moments, basis, slope, loaded, rate_t, root_t, amount_t)
    message = lax.all_to_all(message, "dp", 0, 0, tiled=True)
    local_edge = pl.pallas_call(
        edge_kernel,
        grid=(1,),
        in_specs=[edge_spec(1)] * 3 + [whole((3, 3, width)), whole((8, width)), whole((8, width))],
        out_specs=whole((8, width)),
        out_shape=shape(8, width),
        compiler_params=params,
        name="edge",
    )(query_rows, key_rows, value_rows, short_filter, after, impulse)
    message, local_edge = lax.optimization_barrier((message, local_edge))
    factor = 1.0 / math.sqrt(query_rows.shape[0] * groups * length)
    sent, residue_grad, decay_grad = pl.pallas_call(
        lambda *refs: total_kernel(factor, *refs),
        out_shape=(shape(blocks, CARRY_ROWS, LANES, dtype=BF16), flip, flip),
        compiler_params=small_params,
        name="total",
    )(message, carry.transpose(1, 0, 2))
    carry = lax.all_to_all(sent, "seq", 0, 0, tiled=True)

    names = ("carried",)
    *outs, filter_grad = pl.pallas_call(
        finish_kernel,
        grid=grid,
        in_specs=[tall, filters, flat(8), flat(8)] + [flat(BLOCK)] * 4
        + [chunks(CARRY_ROWS)] + table_specs(names),
        out_specs=[tall] * 3 + [filters],
        out_shape=[jax.ShapeDtypeStruct(query_rows.shape, BF16)] * 3 + [shape(3, 3, width)],
        compiler_params=params,
        name="finish",
    )(
        cotangent, short_filter, after, local_edge, key_short, value_short,
        mixed, grad, carry, *[tables[name] for name in names],
    )
    return (*outs, filter_grad, residue_grad.T, decay_grad.T)


def solution(mesh):
    rows = P("dp", "seq", None)
    return jax.shard_map(
        body,
        mesh=mesh,
        in_specs=(rows, rows, rows, rows, P(), P("seq", None), P("seq", None)),
        out_specs=(rows, rows, rows, P(), P("seq", None), P("seq", None)),
        check_vma=False,
    )
```

```python
import math

import jax
import jax.numpy as jnp
import numpy as np
from jax import lax
from jax.experimental import pallas as pl
from jax.experimental.pallas import tpu as pltpu
from jax.sharding import PartitionSpec as P

BLOCK = 128
CENTRE = BLOCK // 2
TERMS = 10
SHORT_TERMS = 9
PRODUCTS = 9
SENT_ROWS = 128
LAG_ROW = PRODUCTS * SHORT_TERMS
SUM_ROW = 96
CARRY_ROWS = 48
TOP_RATE = 1.0 / 32.0
FREQS = 128
LANES = 128
BF16 = jnp.bfloat16
F32 = jnp.float32
VMEM_LIMIT = 63 * 1024 * 1024
FULL_LIMIT = 64 * 1024 * 1024 - 65536
SMALL_LIMIT = 16 * 1024 * 1024
WIDE = 1024
INNER = 256
SKEW = 2
ORDERED = False


def decay_terms(times, terms=TERMS):
    points = 64
    theta = (np.arange(points) + 0.5) * np.pi / points
    rates = (np.cos(theta) + 1.0) * TOP_RATE / 2.0
    values = np.exp(-np.asarray(times, np.float64)[:, None] * rates[None, :])
    basis = np.cos(np.arange(terms)[None, :] * theta[:, None]) * (2.0 / points)
    basis[:, 0] *= 0.5
    return values @ basis


def halves(table):
    table = np.asarray(table, np.float32)
    high = table.astype(BF16)
    low = (table - high.astype(np.float32)).astype(BF16)
    return high, low


def paired(table):
    return np.concatenate(halves(table), axis=1)


def make_tables():
    t = np.arange(BLOCK)
    angle = 2.0 * np.pi / (2 * FREQS) * (np.arange(FREQS)[:, None] + 0.5) * t[None, :]
    fore = np.concatenate([np.cos(angle), -np.sin(angle)], axis=0)
    back = np.concatenate([np.cos(angle.T), -np.sin(angle.T)], axis=1) / FREQS
    ahead = decay_terms(t - CENTRE)
    behind = decay_terms(CENTRE - t)
    moments = np.zeros((SUM_ROW, (PRODUCTS + 2) * BLOCK))
    for m in range(PRODUCTS):
        part = decay_terms(t - CENTRE if m < 3 else CENTRE - t, SHORT_TERMS).T
        rows = slice(m * SHORT_TERMS, (m + 1) * SHORT_TERMS)
        moments[rows, m * BLOCK : (m + 1) * BLOCK] = part
    moments[LAG_ROW : LAG_ROW + TERMS, PRODUCTS * BLOCK :] = ahead.T @ back
    blank = np.zeros((16 - TERMS, BLOCK))
    taps = np.zeros((16, TERMS))
    taps[:3] = decay_terms([-CENTRE, 1 - CENTRE, -1 - CENTRE])
    edge = np.zeros((16, TERMS))
    edge[:2] = decay_terms([-CENTRE, -1 - CENTRE])

    def padded(table, repeat=0):
        out = np.zeros((table.shape[0], 16))
        out[:, :TERMS] = table
        out[:, TERMS : TERMS + repeat] = table[:, :repeat]
        return out

    first, second = decay_terms([-CENTRE, 1 - CENTRE])

    def tripled(table):
        high, low = halves(padded(table))
        return np.concatenate([high, high, low], axis=1)

    carried = np.zeros((2 * BLOCK + 16, 64))
    carried[:BLOCK, :32] = paired(padded(ahead, 16 - TERMS))
    carried[BLOCK : 2 * BLOCK, 32:] = paired(padded(behind, 16 - TERMS))
    carried[2 * BLOCK :, 32:] = paired(padded(edge, 16 - TERMS))
    return dict(
        moments=moments.astype(BF16),
        fore_u=paired(np.concatenate([fore, behind.T, blank], axis=0)),
        fore_g=paired(np.concatenate([fore, ahead.T, blank], axis=0)),
        impulse=tripled(np.concatenate([fore @ ahead, taps], axis=0)),
        back=back.astype(BF16),
        carried=carried.astype(BF16),
        first=[float(x) for x in first],
        second=[float(x) for x in second],
    )


def dot(left, right):
    return jnp.dot(left, right, preferred_element_type=F32)


def whole(shape):
    return pl.BlockSpec(shape, lambda *_: (0,) * len(shape))


def later_rows(values, before, by):
    moved = pltpu.roll(values, by, 0)
    top = moved[:8]
    row = lax.broadcasted_iota(jnp.int32, top.shape, 0)
    for i in range(by):
        top = jnp.where(row == i, before[2 - by + i : 3 - by + i], top)
    return jnp.concatenate([top, moved[8:]], axis=0)


def sooner_rows(values, after):
    count = values.shape[0]
    moved = pltpu.roll(values, count - 1, 0)
    row = lax.broadcasted_iota(jnp.int32, (8, values.shape[1]), 0)
    bottom = jnp.where(row == 7, after, moved[count - 8 :])
    return jnp.concatenate([moved[: count - 8], bottom], axis=0)


def lanes_of(ref, rows, chunks):
    return jnp.concatenate([ref[i, rows, :] for i in range(chunks.start, chunks.stop)], axis=1)


def store_chunks(ref, chunks, start, rows):
    rows = rows.astype(BF16)
    for i in range(chunks.stop - chunks.start):
        ref[chunks.start + i, start : start + rows.shape[0], :] = rows[:, i * LANES : (i + 1) * LANES]


def edge_rows(skip, refs):
    rows = [ref[0].astype(F32)[skip : skip + 2] for ref in refs]
    rows.extend([jnp.zeros_like(rows[0])] * (4 - len(rows)))
    return jnp.concatenate(rows, axis=0).astype(BF16)


def front_kernel(*refs):
    refs[-1][...] = edge_rows(0, refs[:-1])


def prep_kernel(
    amount_ref, rate_ref, query_ref, key_ref, value_ref,
    root_ref, basis_ref, slope_ref, loaded_ref, spread_ref, last_ref,
):
    last_ref[...] = edge_rows(14, (query_ref, key_ref, value_ref))
    amount, rate = amount_ref[...], rate_ref[...]
    square = rate * rate
    sinh = rate * (1.0 + square * (1.0 / 6.0 + square * (1.0 / 120.0)))
    root = jnp.sqrt(2.0 * jnp.exp(-rate) * sinh)
    root_ref[...] = root
    weight = amount * root
    centred = weight * jnp.exp(-float(CENTRE) * rate)
    spot = rate * (2.0 / TOP_RATE) - 1.0
    value, older = jnp.ones_like(spot), spot
    slope, older_slope = jnp.zeros_like(spot), jnp.zeros_like(spot)
    rows = []
    for k in range(TERMS):
        basis_ref[k] = value
        slope_ref[k] = slope * (-2.0 / TOP_RATE)
        loaded_ref[k] = value * weight
        rows.append(jnp.sum(value * centred, axis=0, keepdims=True))
        if k == 0:
            following, following_slope = spot, jnp.ones_like(spot)
        else:
            following = 2.0 * spot * value - older
            following_slope = 2.0 * value + 2.0 * spot * slope - older_slope
        older, older_slope = value, slope
        value, slope = following, following_slope
    rows.append(jnp.zeros((16 - TERMS, LANES), F32))
    coefs = jnp.concatenate(rows, axis=0)
    high = coefs.astype(BF16)
    low = (coefs - high.astype(F32)).astype(BF16)
    both = jnp.concatenate([high, low], axis=0)
    spread_ref[...] = jnp.broadcast_to(both[None], spread_ref.shape)


def interleave(waiting, skew):
    active, turn = [], 0
    while waiting or active:
        if waiting and turn % skew == 0:
            active.append(waiting.pop(0))
        for steps in list(active):
            if next(steps, active) is active:
                active.remove(steps)
        turn += 1


def block_kernel(
    query_ref, key_ref, value_ref, cot_ref, filter_ref, before_ref, coefs_ref,
    fore_u_ref, fore_g_ref, impulse_ref, back_ref, moments_ref,
    sent_ref, mixed_ref, grad_ref, key_short_ref, value_short_ref, impulse_out, products,
):
    width = mixed_ref.shape[1]
    step = min(INNER, width)
    waiting = [
        block_columns(
            slice(start, start + step), slice(start // LANES, (start + step) // LANES),
            query_ref, key_ref, value_ref, cot_ref, filter_ref, before_ref, coefs_ref,
            fore_u_ref, fore_g_ref, impulse_ref, back_ref, moments_ref,
            sent_ref, mixed_ref, grad_ref, key_short_ref, value_short_ref, impulse_out, products,
        )
        for start in range(0, width, step)
    ]
    interleave(waiting, SKEW)


def block_columns(
    at, chunks,
    query_ref, key_ref, value_ref, cot_ref, filter_ref, before_ref, coefs_ref,
    fore_u_ref, fore_g_ref, impulse_ref, back_ref, moments_ref,
    sent_ref, mixed_ref, grad_ref, key_short_ref, value_short_ref, impulse_out, products,
):
    before = before_ref[:, at].astype(F32)
    query, key, value = (ref[0, :, at].astype(F32) for ref in (query_ref, key_ref, value_ref))
    cot = cot_ref[0, :, at].astype(F32)

    def lagged(i, x):
        edge = before[2 * i : 2 * i + 2]
        return (x, later_rows(x, edge, 1), later_rows(x, edge, 2))

    def short(i, inputs):
        return sum(filter_ref[i, j : j + 1, at] * inputs[j] for j in range(3))

    queries, keys, values = lagged(0, query), lagged(1, key), lagged(2, value)
    key_short, value_short = short(1, keys), short(2, values)
    key_short_ref[:, at] = key_short.astype(BF16)
    value_short_ref[:, at] = value_short.astype(BF16)
    gated = (key_short * value_short).astype(BF16)
    grad_mixed = (cot * short(0, queries)).astype(BF16)
    for i, (left, inputs) in enumerate(((cot, queries), (value_short, keys), (key_short, values))):
        for j in range(3):
            start = (3 * i + j) * BLOCK
            products[start : start + BLOCK, at] = left.astype(BF16) * inputs[j].astype(BF16)

    yield
    u = dot(fore_u_ref[...], jnp.concatenate([gated, gated], axis=0))
    g = dot(fore_g_ref[...], jnp.concatenate([grad_mixed, grad_mixed], axis=0))
    coefs = lanes_of(coefs_ref, slice(None), chunks)
    h = dot(impulse_ref[...], jnp.concatenate([coefs, coefs[:16]], axis=0))
    impulse_out[:, at] = h[2 * FREQS : 2 * FREQS + 8]
    yield
    ur, ui, gr, gi, hr, hi = (
        x[part * FREQS : (part + 1) * FREQS].astype(BF16) for x in (u, g, h) for part in (0, 1)
    )

    def spectrum(real, imag):
        return jnp.concatenate([real.astype(BF16), imag.astype(BF16)], axis=0)

    products[PRODUCTS * BLOCK :, at] = spectrum(gr * ur + gi * ui, gi * ur - gr * ui)
    mixed = dot(back_ref[...], spectrum(ur * hr - ui * hi, ur * hi + ui * hr))
    grad = dot(back_ref[...], spectrum(gr * hr + gi * hi, gi * hr - gr * hi))
    yield
    mixed_ref[:, at] = mixed.astype(BF16)
    grad_ref[:, at] = grad.astype(BF16)
    row = lax.broadcasted_iota(jnp.int32, (16, mixed.shape[1]), 0)
    sums = [u[2 * FREQS :], g[2 * FREQS :]]
    spare = 16 - TERMS
    for i, (inputs, weight) in enumerate(
        ((queries, cot * mixed), (keys, value_short * grad), (values, key_short * grad))
    ):
        for j in range(3):
            m = 3 * i + j
            local = jnp.sum(inputs[j] * weight, axis=0, keepdims=True)
            sums[m // spare] = jnp.where(row == TERMS + m % spare, local, sums[m // spare])
    yield
    store_chunks(sent_ref, chunks, 0, dot(moments_ref[...], products[:, at]))
    store_chunks(sent_ref, chunks, SUM_ROW, sums[0])
    store_chunks(sent_ref, chunks, SUM_ROW + 16, sums[1])


def owner_kernel(
    first, second, moments_ref, basis_ref, slope_ref, loaded_ref, rate_ref, root_ref, amount_ref,
    carry_ref, message_ref, ahead, behind,
):
    blocks = moments_ref.shape[1]
    modes = rate_ref.shape[0]
    row = lax.broadcasted_iota(jnp.int32, (blocks, LANES), 0)
    lag, sum_u, sum_g, spare = LAG_ROW, SUM_ROW, SUM_ROW + 16, 16 - TERMS

    def later(x, by):
        return jnp.where(row >= by, pltpu.roll(x, by, 0), 0.0)

    def sooner(x, by):
        return jnp.where(row < blocks - by, pltpu.roll(x, blocks - by, 0), 0.0)

    lag_rows = [jnp.sum(moments_ref[lag + k], axis=0, keepdims=True) for k in range(TERMS)]
    first_rows, second_rows = [], []
    for n in range(modes):
        basis = [basis_ref[k, n : n + 1, :] for k in range(TERMS)]
        slope = [slope_ref[k, n : n + 1, :] for k in range(TERMS)]
        state = sum(basis[k] * moments_ref[sum_u + k] for k in range(TERMS))
        state_slope = sum(slope[k] * moments_ref[sum_u + k] for k in range(1, TERMS))
        grad = sum(basis[k] * moments_ref[sum_g + k] for k in range(TERMS))
        grad_slope = sum(slope[k] * moments_ref[sum_g + k] for k in range(1, TERMS))
        rate = rate_ref[n : n + 1, :]
        half = jnp.exp(-float(CENTRE) * rate)
        factor = half * half
        moved = later(state, 1)
        forward = factor * moved
        forward_slope = factor * (later(state_slope, 1) + float(BLOCK) * moved)
        backward = factor * sooner(grad, 1)
        by = 1
        while by < blocks:
            moved = later(forward, by)
            forward_slope = forward_slope + factor * (
                later(forward_slope, by) + float(BLOCK * by) * moved
            )
            forward = forward + factor * moved
            backward = backward + factor * sooner(backward, by)
            factor = factor * factor
            by *= 2
        ahead[n] = forward
        behind[n] = backward
        first_sum = jnp.sum(forward * grad, axis=0, keepdims=True)
        second_sum = jnp.sum(forward_slope * grad + forward * grad_slope, axis=0, keepdims=True)
        near = half * sum(basis[k] * lag_rows[k] for k in range(TERMS))
        near_slope = half * sum(slope[k] * lag_rows[k] for k in range(1, TERMS))
        first_rows.append(first_sum + near)
        second_rows.append(second_sum + near_slope + float(CENTRE) * near)
    totals = [moments_ref[SUM_ROW + 16 * (m // spare) + TERMS + m % spare] for m in range(PRODUCTS)]
    edge_one, edge_two = 0.0, 0.0
    for k in range(TERMS):
        carry = sum(loaded_ref[k, n : n + 1, :] * ahead[n] for n in range(modes))
        back = sum(loaded_ref[k, n : n + 1, :] * behind[n] for n in range(modes))
        for start, value in ((0, carry), (16, back)):
            high = value.astype(BF16)
            carry_ref[start + k] = high
            if k < 16 - TERMS:
                carry_ref[start + TERMS + k] = (value - high.astype(F32)).astype(BF16)
        edge_one = edge_one + first[k] * carry
        edge_two = edge_two + second[k] * carry
        if k < SHORT_TERMS:
            for m in range(PRODUCTS):
                totals[m] = totals[m] + (carry if m < 3 else back) * moments_ref[m * SHORT_TERMS + k]
    carry_ref[32] = sooner(edge_one, 1).astype(BF16)
    carry_ref[33] = sooner(edge_two, 1).astype(BF16)
    root, amount = root_ref[...], amount_ref[...]
    first_sum = jnp.concatenate(first_rows, axis=0)
    second_sum = jnp.concatenate(second_rows, axis=0)
    rate = rate_ref[...]
    steep = amount * (jnp.exp(-2.0 * rate) / root * first_sum - root * second_sum)
    for i in range(34, CARRY_ROWS):
        carry_ref[i] = jnp.zeros((blocks, LANES), BF16)
    rows = [jnp.zeros((2, LANES), F32)]
    rows.extend(jnp.sum(total, axis=0, keepdims=True) for total in totals)
    rows.append(jnp.zeros((14 - PRODUCTS, LANES), F32))
    message = jnp.concatenate([*rows, root * first_sum, rate * steep], axis=0)
    message_ref[...] = message


def pair_kernel(own_ref, other_ref, message_ref):
    message = (own_ref[...] + other_ref[...]).astype(BF16)
    message_ref[...] = jnp.broadcast_to(message[None], message_ref.shape)


def total_kernel(factor, message_ref, carry_ref, sent_ref, residue_ref, decay_ref):
    total = message_ref[0].astype(F32)
    for i in range(1, message_ref.shape[0]):
        total = total + message_ref[i].astype(F32)
    total = total * factor
    modes = residue_ref.shape[0]
    residue_ref[...] = total[16 : 16 + modes]
    decay_ref[...] = total[16 + modes :]
    shared = total[:16]
    for block in range(sent_ref.shape[0]):
        sent_ref[block, :32, :] = carry_ref[block, :32, :]
        sent_ref[block, 32:48, :] = (carry_ref[block, 32:48, :].astype(F32) + shared).astype(BF16)


def edge_kernel(query_end, key_end, value_end, filter_ref, after_ref, impulse_ref, edge_ref):
    after, impulse = after_ref[...].astype(F32), impulse_ref[...]

    def rounded(x):
        return x.astype(BF16).astype(F32)

    def short_after(i, ref):
        last, following = ref[0].astype(F32)[14:], after[2 * i : 2 * i + 2]
        middle = jnp.concatenate([last[1:2], following[0:1]], axis=0)
        zero, one, two = (filter_ref[i, j : j + 1, :] for j in range(3))
        return zero * following + one * middle + two * last

    query_next, key_next, value_next = (
        short_after(i, ref) for i, ref in enumerate((query_end, key_end, value_end))
    )
    gated_next = rounded(key_next * value_next)
    grad_mixed_next = rounded(after[6:7] * query_next[0:1])
    edge_ref[...] = jnp.concatenate(
        [
            impulse[0:1] * gated_next[0:1],
            impulse[0:1] * gated_next[1:2] + impulse[1:2] * gated_next[0:1],
            -impulse[2:3] * grad_mixed_next,
            jnp.zeros_like(grad_mixed_next),
            key_next,
            value_next,
        ],
        axis=0,
    )


def finish_kernel(
    cot_ref, filter_ref, after_ref, local_edge_ref, key_short_ref, value_short_ref,
    mixed_ref, grad_ref, carry_ref, carried_ref,
    query_out, key_out, value_out, filter_out,
):
    step = min(INNER, mixed_ref.shape[1])
    for start in range(0, mixed_ref.shape[1], step):
        finish_columns(
            slice(start, start + step), slice(start // LANES, (start + step) // LANES),
            cot_ref, filter_ref, after_ref, local_edge_ref, key_short_ref, value_short_ref,
            mixed_ref, grad_ref, carry_ref, carried_ref,
            query_out, key_out, value_out, filter_out,
        )


def finish_columns(
    at, chunks,
    cot_ref, filter_ref, after_ref, local_edge_ref, key_short_ref, value_short_ref,
    mixed_ref, grad_ref, carry_ref, carried_ref,
    query_out, key_out, value_out, filter_out,
):
    after, local_edge = after_ref[:, at].astype(F32), local_edge_ref[:, at]

    def tap(i, j):
        return filter_ref[i, j : j + 1, at]

    both = lanes_of(carry_ref, slice(0, 32), chunks)
    both = jnp.concatenate([both[:16], both[:16], both[16:], both[16:]], axis=0)
    carried = dot(carried_ref[...], both)
    rest = lanes_of(carry_ref, slice(32, 48), chunks).astype(F32)
    for m in range(PRODUCTS):
        filter_out[m // 3, m % 3 : m % 3 + 1, at] = rest[2 + m : 3 + m]
    mixed = mixed_ref[:, at].astype(F32) + carried[:BLOCK]
    grad = grad_ref[:, at].astype(F32) + carried[BLOCK : 2 * BLOCK]
    edge = carried[2 * BLOCK :]
    mixed_next = rest[0:1] + local_edge[0:1], rest[1:2] + local_edge[1:2]
    grad_next = edge[0:1], edge[1:2] + local_edge[2:3]

    cot = cot_ref[0, :, at].astype(F32)
    for i, (out_ref, left, right, left_next, right_next) in enumerate(
        (
            (query_out, cot, mixed, after[6:8], mixed_next),
            (key_out, value_short_ref[:, at].astype(F32), grad, local_edge[6:8], grad_next),
            (value_out, key_short_ref[:, at].astype(F32), grad, local_edge[4:6], grad_next),
        )
    ):
        zero, one, two = (tap(i, j) for j in range(3))
        here = left * right
        following = left_next[0:1] * right_next[0]
        inner = one * here + sooner_rows(two * here, two * following)
        inner_after = one * following + two * (left_next[1:2] * right_next[1])
        out_ref[0, :, at] = (zero * here + sooner_rows(inner, inner_after)).astype(BF16)


def body(query_rows, key_rows, value_rows, cotangent, short_filter, residue, decay_rate):
    width = query_rows.shape[2]
    blocks = lax.axis_size("seq")
    groups = lax.axis_size("dp")
    modes = residue.shape[1]
    length = BLOCK * blocks
    wide = min(WIDE, width)
    parts = wide // LANES
    grid = (width // wide,)
    tables = make_tables()
    first, second = tables.pop("first"), tables.pop("second")
    tables = {name: jnp.asarray(table) for name, table in tables.items()}
    params = pltpu.CompilerParams(vmem_limit_bytes=VMEM_LIMIT)
    full_params = pltpu.CompilerParams(vmem_limit_bytes=FULL_LIMIT)
    small_params = pltpu.CompilerParams(vmem_limit_bytes=SMALL_LIMIT)

    def shape(*dims, dtype=F32):
        return jax.ShapeDtypeStruct(dims, dtype)

    def edge_spec(end):
        return pl.BlockSpec((1, 16, width), lambda c: (0, (BLOCK // 16 - 1) * end, 0))

    flip, small = shape(modes, LANES), shape(TERMS, modes, LANES)
    amount_t, rate_t = residue.T, decay_rate.T
    edges = shape(8, width, dtype=BF16)
    outs = (flip, small, small, small, shape(blocks, 32, LANES, dtype=BF16), edges)
    root_t, basis, slope, loaded, spread, last = pl.pallas_call(
        prep_kernel,
        grid=(1,),
        in_specs=[whole(flip.shape)] * 2 + [edge_spec(1)] * 3,
        out_specs=[whole(out.shape) for out in outs],
        out_shape=outs,
        compiler_params=params,
        name="prep",
    )(amount_t, rate_t, query_rows, key_rows, value_rows)
    before = lax.ppermute(last, "seq", [(i, i + 1) for i in range(blocks - 1)])
    coefs = lax.all_to_all(spread, "seq", 0, 0, tiled=True)

    tall = pl.BlockSpec((1, BLOCK, wide), lambda c: (0, 0, c))
    filters = pl.BlockSpec((3, 3, wide), lambda c: (0, 0, c))

    def flat(rows):
        return pl.BlockSpec((rows, wide), lambda c: (0, c))

    def chunks(rows):
        return pl.BlockSpec((parts, rows, LANES), lambda c: (c, 0, 0))

    def table_specs(names):
        return [whole(tables[name].shape) for name in names]

    names = ("fore_u", "fore_g", "impulse", "back", "moments")
    half = shape(BLOCK, width, dtype=BF16)
    sent, mixed, grad, key_short, value_short, impulse = pl.pallas_call(
        block_kernel,
        grid=grid,
        in_specs=[tall] * 4 + [filters, flat(8), chunks(32)] + table_specs(names),
        out_specs=(chunks(SENT_ROWS), *[flat(BLOCK)] * 4, flat(8)),
        out_shape=(shape(blocks, SENT_ROWS, LANES, dtype=BF16), half, half, half, half, shape(8, width)),
        scratch_shapes=[pltpu.VMEM(((PRODUCTS + 2) * BLOCK, wide), BF16)],
        compiler_params=full_params,
        name="block",
    )(
        query_rows, key_rows, value_rows, cotangent, short_filter, before, coefs,
        *[tables[name] for name in names],
    )
    front = pl.pallas_call(
        front_kernel,
        grid=(1,),
        in_specs=[edge_spec(0)] * 4,
        out_specs=whole((8, width)),
        out_shape=edges,
        compiler_params=params,
        name="front",
    )(query_rows, key_rows, value_rows, cotangent)
    sent, front = lax.optimization_barrier((sent, front))
    moments = lax.all_to_all(sent, "seq", 0, 0, tiled=True)
    after = lax.ppermute(front, "seq", [(i + 1, i) for i in range(blocks - 1)])
    moments, after = lax.optimization_barrier((moments, after))
    moments = moments.transpose(1, 0, 2).astype(F32)

    carry, message = pl.pallas_call(
        lambda *refs: owner_kernel(first, second, *refs),
        out_shape=(
            shape(CARRY_ROWS, blocks, LANES, dtype=BF16),
            shape(16 + 2 * modes, LANES),
        ),
        scratch_shapes=[pltpu.VMEM((modes, blocks, LANES), F32)] * 2,
        compiler_params=small_params,
        name="owner",
    )(moments, basis, slope, loaded, rate_t, root_t, amount_t)
    other = lax.ppermute(message, "dp", [(i, i ^ 1) for i in range(groups)])
    message = pl.pallas_call(
        pair_kernel,
        out_shape=shape(groups // 2, 16 + 2 * modes, LANES, dtype=BF16),
        compiler_params=small_params,
        name="pair",
    )(message, other)
    alike = [list(range(i, groups, 2)) for i in range(2)]
    message = lax.all_to_all(message, "dp", 0, 0, axis_index_groups=alike, tiled=True)
    local_edge = pl.pallas_call(
        edge_kernel,
        grid=(1,),
        in_specs=[edge_spec(1)] * 3 + [whole((3, 3, width)), whole((8, width)), whole((8, width))],
        out_specs=whole((8, width)),
        out_shape=shape(8, width),
        compiler_params=params,
        name="edge",
    )(query_rows, key_rows, value_rows, short_filter, after, impulse)
    message, local_edge = lax.optimization_barrier((message, local_edge))
    factor = 1.0 / math.sqrt(query_rows.shape[0] * groups * length)
    sent, residue_grad, decay_grad = pl.pallas_call(
        lambda *refs: total_kernel(factor, *refs),
        out_shape=(shape(blocks, CARRY_ROWS, LANES, dtype=BF16), flip, flip),
        compiler_params=small_params,
        name="total",
    )(message, carry.transpose(1, 0, 2))
    carry = lax.all_to_all(sent, "seq", 0, 0, tiled=True)

    names = ("carried",)
    *outs, filter_grad = pl.pallas_call(
        finish_kernel,
        grid=grid,
        in_specs=[tall, filters, flat(8), flat(8)] + [flat(BLOCK)] * 4
        + [chunks(CARRY_ROWS)] + table_specs(names),
        out_specs=[tall] * 3 + [filters],
        out_shape=[jax.ShapeDtypeStruct(query_rows.shape, BF16)] * 3 + [shape(3, 3, width)],
        compiler_params=params,
        name="finish",
    )(
        cotangent, short_filter, after, local_edge, key_short, value_short,
        mixed, grad, carry, *[tables[name] for name in names],
    )
    return (*outs, filter_grad, residue_grad.T, decay_grad.T)


def solution(mesh):
    rows = P("dp", "seq", None)
    return jax.shard_map(
        body,
        mesh=mesh,
        in_specs=(rows, rows, rows, rows, P(), P("seq", None), P("seq", None)),
        out_specs=(rows, rows, rows, P(), P("seq", None), P("seq", None)),
        check_vma=False,
    )
```

```python
import math

import jax
import jax.numpy as jnp
import numpy as np
from jax import lax
from jax.experimental import pallas as pl
from jax.experimental.pallas import tpu as pltpu
from jax.sharding import PartitionSpec as P

BLOCK = 128
CENTRE = BLOCK // 2
TERMS = 10
SHORT_TERMS = 9
PRODUCTS = 9
SENT_ROWS = 128
LAG_ROW = PRODUCTS * SHORT_TERMS
SUM_ROW = 96
CARRY_ROWS = 48
TOP_RATE = 1.0 / 32.0
FREQS = 128
LANES = 128
BF16 = jnp.bfloat16
F32 = jnp.float32
VMEM_LIMIT = 63 * 1024 * 1024
FULL_LIMIT = 64 * 1024 * 1024 - 65536
SMALL_LIMIT = 16 * 1024 * 1024
WIDE = 1024
INNER = 256
SKEW = 2
ORDERED = False


def decay_terms(times, terms=TERMS):
    points = 64
    theta = (np.arange(points) + 0.5) * np.pi / points
    rates = (np.cos(theta) + 1.0) * TOP_RATE / 2.0
    values = np.exp(-np.asarray(times, np.float64)[:, None] * rates[None, :])
    basis = np.cos(np.arange(terms)[None, :] * theta[:, None]) * (2.0 / points)
    basis[:, 0] *= 0.5
    return values @ basis


def halves(table):
    table = np.asarray(table, np.float32)
    high = table.astype(BF16)
    low = (table - high.astype(np.float32)).astype(BF16)
    return high, low


def paired(table):
    return np.concatenate(halves(table), axis=1)


def make_tables():
    t = np.arange(BLOCK)
    angle = 2.0 * np.pi / (2 * FREQS) * (np.arange(FREQS)[:, None] + 0.5) * t[None, :]
    fore = np.concatenate([np.cos(angle), -np.sin(angle)], axis=0)
    back = np.concatenate([np.cos(angle.T), -np.sin(angle.T)], axis=1) / FREQS
    ahead = decay_terms(t - CENTRE)
    behind = decay_terms(CENTRE - t)
    moments = np.zeros((SUM_ROW, (PRODUCTS + 2) * BLOCK))
    for m in range(PRODUCTS):
        part = decay_terms(t - CENTRE if m < 3 else CENTRE - t, SHORT_TERMS).T
        rows = slice(m * SHORT_TERMS, (m + 1) * SHORT_TERMS)
        moments[rows, m * BLOCK : (m + 1) * BLOCK] = part
    moments[LAG_ROW : LAG_ROW + TERMS, PRODUCTS * BLOCK :] = ahead.T @ back
    blank = np.zeros((16 - TERMS, BLOCK))
    taps = np.zeros((16, TERMS))
    taps[:3] = decay_terms([-CENTRE, 1 - CENTRE, -1 - CENTRE])
    edge = np.zeros((16, TERMS))
    edge[:2] = decay_terms([-CENTRE, -1 - CENTRE])

    def padded(table, repeat=0):
        out = np.zeros((table.shape[0], 16))
        out[:, :TERMS] = table
        out[:, TERMS : TERMS + repeat] = table[:, :repeat]
        return out

    first, second = decay_terms([-CENTRE, 1 - CENTRE])

    def tripled(table):
        high, low = halves(padded(table))
        return np.concatenate([high, high, low], axis=1)

    carried = np.zeros((2 * BLOCK + 16, 64))
    carried[:BLOCK, :32] = paired(padded(ahead, 16 - TERMS))
    carried[BLOCK : 2 * BLOCK, 32:] = paired(padded(behind, 16 - TERMS))
    carried[2 * BLOCK :, 32:] = paired(padded(edge, 16 - TERMS))
    return dict(
        moments=moments.astype(BF16),
        fore_u=paired(np.concatenate([fore, behind.T, blank], axis=0)),
        fore_g=paired(np.concatenate([fore, ahead.T, blank], axis=0)),
        impulse=tripled(np.concatenate([fore @ ahead, taps], axis=0)),
        back=back.astype(BF16),
        carried=carried.astype(BF16),
        first=[float(x) for x in first],
        second=[float(x) for x in second],
    )


def dot(left, right):
    return jnp.dot(left, right, preferred_element_type=F32)


def whole(shape):
    return pl.BlockSpec(shape, lambda *_: (0,) * len(shape))


def later_rows(values, before, by):
    moved = pltpu.roll(values, by, 0)
    top = moved[:8]
    row = lax.broadcasted_iota(jnp.int32, top.shape, 0)
    for i in range(by):
        top = jnp.where(row == i, before[2 - by + i : 3 - by + i], top)
    return jnp.concatenate([top, moved[8:]], axis=0)


def sooner_rows(values, after):
    count = values.shape[0]
    moved = pltpu.roll(values, count - 1, 0)
    row = lax.broadcasted_iota(jnp.int32, (8, values.shape[1]), 0)
    bottom = jnp.where(row == 7, after, moved[count - 8 :])
    return jnp.concatenate([moved[: count - 8], bottom], axis=0)


def lanes_of(ref, rows, chunks):
    return jnp.concatenate([ref[i, rows, :] for i in range(chunks.start, chunks.stop)], axis=1)


def store_chunks(ref, chunks, start, rows):
    rows = rows.astype(BF16)
    for i in range(chunks.stop - chunks.start):
        ref[chunks.start + i, start : start + rows.shape[0], :] = rows[:, i * LANES : (i + 1) * LANES]


def edge_rows(skip, refs):
    rows = [ref[0].astype(F32)[skip : skip + 2] for ref in refs]
    rows.extend([jnp.zeros_like(rows[0])] * (4 - len(rows)))
    return jnp.concatenate(rows, axis=0).astype(BF16)


def front_kernel(*refs):
    refs[-1][...] = edge_rows(0, refs[:-1])


def prep_kernel(
    amount_ref, rate_ref, query_ref, key_ref, value_ref,
    root_ref, basis_ref, slope_ref, loaded_ref, spread_ref, last_ref,
):
    last_ref[...] = edge_rows(14, (query_ref, key_ref, value_ref))
    amount, rate = amount_ref[...], rate_ref[...]
    square = rate * rate
    sinh = rate * (1.0 + square * (1.0 / 6.0 + square * (1.0 / 120.0)))
    root = jnp.sqrt(2.0 * jnp.exp(-rate) * sinh)
    root_ref[...] = root
    weight = amount * root
    centred = weight * jnp.exp(-float(CENTRE) * rate)
    spot = rate * (2.0 / TOP_RATE) - 1.0
    value, older = jnp.ones_like(spot), spot
    slope, older_slope = jnp.zeros_like(spot), jnp.zeros_like(spot)
    rows = []
    for k in range(TERMS):
        basis_ref[k] = value
        slope_ref[k] = slope * (-2.0 / TOP_RATE)
        loaded_ref[k] = value * weight
        rows.append(jnp.sum(value * centred, axis=0, keepdims=True))
        if k == 0:
            following, following_slope = spot, jnp.ones_like(spot)
        else:
            following = 2.0 * spot * value - older
            following_slope = 2.0 * value + 2.0 * spot * slope - older_slope
        older, older_slope = value, slope
        value, slope = following, following_slope
    rows.append(jnp.zeros((16 - TERMS, LANES), F32))
    coefs = jnp.concatenate(rows, axis=0)
    high = coefs.astype(BF16)
    low = (coefs - high.astype(F32)).astype(BF16)
    both = jnp.concatenate([high, low], axis=0)
    spread_ref[...] = jnp.broadcast_to(both[None], spread_ref.shape)


def interleave(waiting, skew):
    active, turn = [], 0
    while waiting or active:
        if waiting and turn % skew == 0:
            active.append(waiting.pop(0))
        for steps in list(active):
            if next(steps, active) is active:
                active.remove(steps)
        turn += 1


def block_kernel(
    query_ref, key_ref, value_ref, cot_ref, filter_ref, before_ref, coefs_ref,
    fore_u_ref, fore_g_ref, impulse_ref, back_ref, moments_ref,
    sent_ref, mixed_ref, grad_ref, key_short_ref, value_short_ref, impulse_out, products,
):
    width = mixed_ref.shape[1]
    step = min(INNER, width)
    waiting = [
        block_columns(
            slice(start, start + step), slice(start // LANES, (start + step) // LANES),
            query_ref, key_ref, value_ref, cot_ref, filter_ref, before_ref, coefs_ref,
            fore_u_ref, fore_g_ref, impulse_ref, back_ref, moments_ref,
            sent_ref, mixed_ref, grad_ref, key_short_ref, value_short_ref, impulse_out, products,
        )
        for start in range(0, width, step)
    ]
    interleave(waiting, SKEW)


def block_columns(
    at, chunks,
    query_ref, key_ref, value_ref, cot_ref, filter_ref, before_ref, coefs_ref,
    fore_u_ref, fore_g_ref, impulse_ref, back_ref, moments_ref,
    sent_ref, mixed_ref, grad_ref, key_short_ref, value_short_ref, impulse_out, products,
):
    before = before_ref[:, at].astype(F32)
    query, key, value = (ref[0, :, at].astype(F32) for ref in (query_ref, key_ref, value_ref))
    cot = cot_ref[0, :, at].astype(F32)

    def lagged(i, x):
        edge = before[2 * i : 2 * i + 2]
        return (x, later_rows(x, edge, 1), later_rows(x, edge, 2))

    def short(i, inputs):
        return sum(filter_ref[i, j : j + 1, at] * inputs[j] for j in range(3))

    queries, keys, values = lagged(0, query), lagged(1, key), lagged(2, value)
    key_short, value_short = short(1, keys), short(2, values)
    key_short_ref[:, at] = key_short.astype(BF16)
    value_short_ref[:, at] = value_short.astype(BF16)
    gated = (key_short * value_short).astype(BF16)
    grad_mixed = (cot * short(0, queries)).astype(BF16)
    for i, (left, inputs) in enumerate(((cot, queries), (value_short, keys), (key_short, values))):
        for j in range(3):
            start = (3 * i + j) * BLOCK
            products[start : start + BLOCK, at] = left.astype(BF16) * inputs[j].astype(BF16)

    yield
    u = dot(fore_u_ref[...], jnp.concatenate([gated, gated], axis=0))
    g = dot(fore_g_ref[...], jnp.concatenate([grad_mixed, grad_mixed], axis=0))
    coefs = lanes_of(coefs_ref, slice(None), chunks)
    h = dot(impulse_ref[...], jnp.concatenate([coefs, coefs[:16]], axis=0))
    impulse_out[:, at] = h[2 * FREQS : 2 * FREQS + 8]
    yield
    ur, ui, gr, gi, hr, hi = (
        x[part * FREQS : (part + 1) * FREQS].astype(BF16) for x in (u, g, h) for part in (0, 1)
    )

    def spectrum(real, imag):
        return jnp.concatenate([real.astype(BF16), imag.astype(BF16)], axis=0)

    products[PRODUCTS * BLOCK :, at] = spectrum(gr * ur + gi * ui, gi * ur - gr * ui)
    mixed = dot(back_ref[...], spectrum(ur * hr - ui * hi, ur * hi + ui * hr))
    grad = dot(back_ref[...], spectrum(gr * hr + gi * hi, gi * hr - gr * hi))
    yield
    mixed_ref[:, at] = mixed.astype(BF16)
    grad_ref[:, at] = grad.astype(BF16)
    row = lax.broadcasted_iota(jnp.int32, (16, mixed.shape[1]), 0)
    sums = [u[2 * FREQS :], g[2 * FREQS :]]
    spare = 16 - TERMS
    for i, (inputs, weight) in enumerate(
        ((queries, cot * mixed), (keys, value_short * grad), (values, key_short * grad))
    ):
        for j in range(3):
            m = 3 * i + j
            local = jnp.sum(inputs[j] * weight, axis=0, keepdims=True)
            sums[m // spare] = jnp.where(row == TERMS + m % spare, local, sums[m // spare])
    yield
    store_chunks(sent_ref, chunks, 0, dot(moments_ref[...], products[:, at]))
    store_chunks(sent_ref, chunks, SUM_ROW, sums[0])
    store_chunks(sent_ref, chunks, SUM_ROW + 16, sums[1])


def owner_kernel(
    first, second, moments_ref, basis_ref, slope_ref, loaded_ref, rate_ref, root_ref, amount_ref,
    carry_ref, message_ref, ahead, behind,
):
    blocks = moments_ref.shape[1]
    modes = rate_ref.shape[0]
    row = lax.broadcasted_iota(jnp.int32, (blocks, LANES), 0)
    lag, sum_u, sum_g, spare = LAG_ROW, SUM_ROW, SUM_ROW + 16, 16 - TERMS

    def later(x, by):
        return jnp.where(row >= by, pltpu.roll(x, by, 0), 0.0)

    def sooner(x, by):
        return jnp.where(row < blocks - by, pltpu.roll(x, blocks - by, 0), 0.0)

    lag_rows = [jnp.sum(moments_ref[lag + k], axis=0, keepdims=True) for k in range(TERMS)]
    first_rows, second_rows = [], []
    for n in range(modes):
        basis = [basis_ref[k, n : n + 1, :] for k in range(TERMS)]
        slope = [slope_ref[k, n : n + 1, :] for k in range(TERMS)]
        state = sum(basis[k] * moments_ref[sum_u + k] for k in range(TERMS))
        state_slope = sum(slope[k] * moments_ref[sum_u + k] for k in range(1, TERMS))
        grad = sum(basis[k] * moments_ref[sum_g + k] for k in range(TERMS))
        grad_slope = sum(slope[k] * moments_ref[sum_g + k] for k in range(1, TERMS))
        rate = rate_ref[n : n + 1, :]
        half = jnp.exp(-float(CENTRE) * rate)
        factor = half * half
        moved = later(state, 1)
        forward = factor * moved
        forward_slope = factor * (later(state_slope, 1) + float(BLOCK) * moved)
        backward = factor * sooner(grad, 1)
        by = 1
        while by < blocks:
            moved = later(forward, by)
            forward_slope = forward_slope + factor * (
                later(forward_slope, by) + float(BLOCK * by) * moved
            )
            forward = forward + factor * moved
            backward = backward + factor * sooner(backward, by)
            factor = factor * factor
            by *= 2
        ahead[n] = forward
        behind[n] = backward
        first_sum = jnp.sum(forward * grad, axis=0, keepdims=True)
        second_sum = jnp.sum(forward_slope * grad + forward * grad_slope, axis=0, keepdims=True)
        near = half * sum(basis[k] * lag_rows[k] for k in range(TERMS))
        near_slope = half * sum(slope[k] * lag_rows[k] for k in range(1, TERMS))
        first_rows.append(first_sum + near)
        second_rows.append(second_sum + near_slope + float(CENTRE) * near)
    totals = [moments_ref[SUM_ROW + 16 * (m // spare) + TERMS + m % spare] for m in range(PRODUCTS)]
    edge_one, edge_two = 0.0, 0.0
    for k in range(TERMS):
        carry = sum(loaded_ref[k, n : n + 1, :] * ahead[n] for n in range(modes))
        back = sum(loaded_ref[k, n : n + 1, :] * behind[n] for n in range(modes))
        for start, value in ((0, carry), (16, back)):
            high = value.astype(BF16)
            carry_ref[start + k] = high
            if k < 16 - TERMS:
                carry_ref[start + TERMS + k] = (value - high.astype(F32)).astype(BF16)
        edge_one = edge_one + first[k] * carry
        edge_two = edge_two + second[k] * carry
        if k < SHORT_TERMS:
            for m in range(PRODUCTS):
                totals[m] = totals[m] + (carry if m < 3 else back) * moments_ref[m * SHORT_TERMS + k]
    carry_ref[32] = sooner(edge_one, 1).astype(BF16)
    carry_ref[33] = sooner(edge_two, 1).astype(BF16)
    root, amount = root_ref[...], amount_ref[...]
    first_sum = jnp.concatenate(first_rows, axis=0)
    second_sum = jnp.concatenate(second_rows, axis=0)
    rate = rate_ref[...]
    steep = amount * (jnp.exp(-2.0 * rate) / root * first_sum - root * second_sum)
    for i in range(34, CARRY_ROWS):
        carry_ref[i] = jnp.zeros((blocks, LANES), BF16)
    rows = [jnp.zeros((2, LANES), F32)]
    rows.extend(jnp.sum(total, axis=0, keepdims=True) for total in totals)
    rows.append(jnp.zeros((14 - PRODUCTS, LANES), F32))
    message = jnp.concatenate([*rows, root * first_sum, rate * steep], axis=0).astype(BF16)
    message_ref[...] = jnp.broadcast_to(message[None], message_ref.shape)


def total_kernel(factor, message_ref, carry_ref, sent_ref, residue_ref, decay_ref):
    total = message_ref[0].astype(F32)
    for i in range(1, message_ref.shape[0]):
        total = total + message_ref[i].astype(F32)
    total = total * factor
    modes = residue_ref.shape[0]
    residue_ref[...] = total[16 : 16 + modes]
    decay_ref[...] = total[16 + modes :]
    shared = total[:16]
    for block in range(sent_ref.shape[0]):
        sent_ref[block, :32, :] = carry_ref[block, :32, :]
        sent_ref[block, 32:48, :] = (carry_ref[block, 32:48, :].astype(F32) + shared).astype(BF16)


def edge_kernel(query_end, key_end, value_end, filter_ref, after_ref, impulse_ref, edge_ref):
    after, impulse = after_ref[...].astype(F32), impulse_ref[...]

    def rounded(x):
        return x.astype(BF16).astype(F32)

    def short_after(i, ref):
        last, following = ref[0].astype(F32)[14:], after[2 * i : 2 * i + 2]
        middle = jnp.concatenate([last[1:2], following[0:1]], axis=0)
        zero, one, two = (filter_ref[i, j : j + 1, :] for j in range(3))
        return zero * following + one * middle + two * last

    query_next, key_next, value_next = (
        short_after(i, ref) for i, ref in enumerate((query_end, key_end, value_end))
    )
    gated_next = rounded(key_next * value_next)
    grad_mixed_next = rounded(after[6:7] * query_next[0:1])
    edge_ref[...] = jnp.concatenate(
        [
            impulse[0:1] * gated_next[0:1],
            impulse[0:1] * gated_next[1:2] + impulse[1:2] * gated_next[0:1],
            -impulse[2:3] * grad_mixed_next,
            jnp.zeros_like(grad_mixed_next),
            key_next,
            value_next,
        ],
        axis=0,
    )


def finish_kernel(
    cot_ref, filter_ref, after_ref, local_edge_ref, key_short_ref, value_short_ref,
    mixed_ref, grad_ref, carry_ref, carried_ref,
    query_out, key_out, value_out, filter_out,
):
    step = mixed_ref.shape[1]
    for start in range(0, mixed_ref.shape[1], step):
        finish_columns(
            slice(start, start + step), slice(start // LANES, (start + step) // LANES),
            cot_ref, filter_ref, after_ref, local_edge_ref, key_short_ref, value_short_ref,
            mixed_ref, grad_ref, carry_ref, carried_ref,
            query_out, key_out, value_out, filter_out,
        )


def finish_columns(
    at, chunks,
    cot_ref, filter_ref, after_ref, local_edge_ref, key_short_ref, value_short_ref,
    mixed_ref, grad_ref, carry_ref, carried_ref,
    query_out, key_out, value_out, filter_out,
):
    after, local_edge = after_ref[:, at].astype(F32), local_edge_ref[:, at]

    def tap(i, j):
        return filter_ref[i, j : j + 1, at]

    both = lanes_of(carry_ref, slice(0, 32), chunks)
    both = jnp.concatenate([both[:16], both[:16], both[16:], both[16:]], axis=0)
    carried = dot(carried_ref[...], both)
    rest = lanes_of(carry_ref, slice(32, 48), chunks).astype(F32)
    for m in range(PRODUCTS):
        filter_out[m // 3, m % 3 : m % 3 + 1, at] = rest[2 + m : 3 + m]
    mixed = mixed_ref[:, at].astype(F32) + carried[:BLOCK]
    grad = grad_ref[:, at].astype(F32) + carried[BLOCK : 2 * BLOCK]
    edge = carried[2 * BLOCK :]
    mixed_next = rest[0:1] + local_edge[0:1], rest[1:2] + local_edge[1:2]
    grad_next = edge[0:1], edge[1:2] + local_edge[2:3]

    cot = cot_ref[0, :, at].astype(F32)
    for i, (out_ref, left, right, left_next, right_next) in enumerate(
        (
            (query_out, cot, mixed, after[6:8], mixed_next),
            (key_out, value_short_ref[:, at].astype(F32), grad, local_edge[6:8], grad_next),
            (value_out, key_short_ref[:, at].astype(F32), grad, local_edge[4:6], grad_next),
        )
    ):
        zero, one, two = (tap(i, j) for j in range(3))
        here = left * right
        following = left_next[0:1] * right_next[0]
        inner = one * here + sooner_rows(two * here, two * following)
        inner_after = one * following + two * (left_next[1:2] * right_next[1])
        out_ref[0, :, at] = (zero * here + sooner_rows(inner, inner_after)).astype(BF16)


def body(query_rows, key_rows, value_rows, cotangent, short_filter, residue, decay_rate):
    width = query_rows.shape[2]
    blocks = lax.axis_size("seq")
    groups = lax.axis_size("dp")
    modes = residue.shape[1]
    length = BLOCK * blocks
    wide = min(WIDE, width)
    parts = wide // LANES
    grid = (width // wide,)
    tables = make_tables()
    first, second = tables.pop("first"), tables.pop("second")
    tables = {name: jnp.asarray(table) for name, table in tables.items()}
    params = pltpu.CompilerParams(vmem_limit_bytes=VMEM_LIMIT)
    full_params = pltpu.CompilerParams(vmem_limit_bytes=FULL_LIMIT)
    small_params = pltpu.CompilerParams(vmem_limit_bytes=SMALL_LIMIT)

    def shape(*dims, dtype=F32):
        return jax.ShapeDtypeStruct(dims, dtype)

    def edge_spec(end):
        return pl.BlockSpec((1, 16, width), lambda c: (0, (BLOCK // 16 - 1) * end, 0))

    flip, small = shape(modes, LANES), shape(TERMS, modes, LANES)
    amount_t, rate_t = residue.T, decay_rate.T
    edges = shape(8, width, dtype=BF16)
    outs = (flip, small, small, small, shape(blocks, 32, LANES, dtype=BF16), edges)
    root_t, basis, slope, loaded, spread, last = pl.pallas_call(
        prep_kernel,
        grid=(1,),
        in_specs=[whole(flip.shape)] * 2 + [edge_spec(1)] * 3,
        out_specs=[whole(out.shape) for out in outs],
        out_shape=outs,
        compiler_params=params,
        name="prep",
    )(amount_t, rate_t, query_rows, key_rows, value_rows)
    before = lax.ppermute(last, "seq", [(i, i + 1) for i in range(blocks - 1)])
    coefs = lax.all_to_all(spread, "seq", 0, 0, tiled=True)

    tall = pl.BlockSpec((1, BLOCK, wide), lambda c: (0, 0, c))
    filters = pl.BlockSpec((3, 3, wide), lambda c: (0, 0, c))

    def flat(rows):
        return pl.BlockSpec((rows, wide), lambda c: (0, c))

    def chunks(rows):
        return pl.BlockSpec((parts, rows, LANES), lambda c: (c, 0, 0))

    def table_specs(names):
        return [whole(tables[name].shape) for name in names]

    names = ("fore_u", "fore_g", "impulse", "back", "moments")
    half = shape(BLOCK, width, dtype=BF16)
    sent, mixed, grad, key_short, value_short, impulse = pl.pallas_call(
        block_kernel,
        grid=grid,
        in_specs=[tall] * 4 + [filters, flat(8), chunks(32)] + table_specs(names),
        out_specs=(chunks(SENT_ROWS), *[flat(BLOCK)] * 4, flat(8)),
        out_shape=(shape(blocks, SENT_ROWS, LANES, dtype=BF16), half, half, half, half, shape(8, width)),
        scratch_shapes=[pltpu.VMEM(((PRODUCTS + 2) * BLOCK, wide), BF16)],
        compiler_params=full_params,
        name="block",
    )(
        query_rows, key_rows, value_rows, cotangent, short_filter, before, coefs,
        *[tables[name] for name in names],
    )
    front = pl.pallas_call(
        front_kernel,
        grid=(1,),
        in_specs=[edge_spec(0)] * 4,
        out_specs=whole((8, width)),
        out_shape=edges,
        compiler_params=params,
        name="front",
    )(query_rows, key_rows, value_rows, cotangent)
    sent, front = lax.optimization_barrier((sent, front))
    moments = lax.all_to_all(sent, "seq", 0, 0, tiled=True)
    after = lax.ppermute(front, "seq", [(i + 1, i) for i in range(blocks - 1)])
    moments, after = lax.optimization_barrier((moments, after))
    moments = moments.transpose(1, 0, 2).astype(F32)

    carry, message = pl.pallas_call(
        lambda *refs: owner_kernel(first, second, *refs),
        out_shape=(
            shape(CARRY_ROWS, blocks, LANES, dtype=BF16),
            shape(groups, 16 + 2 * modes, LANES, dtype=BF16),
        ),
        scratch_shapes=[pltpu.VMEM((modes, blocks, LANES), F32)] * 2,
        compiler_params=small_params,
        name="owner",
    )(moments, basis, slope, loaded, rate_t, root_t, amount_t)
    message = lax.all_to_all(message, "dp", 0, 0, tiled=True)
    local_edge = pl.pallas_call(
        edge_kernel,
        grid=(1,),
        in_specs=[edge_spec(1)] * 3 + [whole((3, 3, width)), whole((8, width)), whole((8, width))],
        out_specs=whole((8, width)),
        out_shape=shape(8, width),
        compiler_params=params,
        name="edge",
    )(query_rows, key_rows, value_rows, short_filter, after, impulse)
    message, local_edge = lax.optimization_barrier((message, local_edge))
    factor = 1.0 / math.sqrt(query_rows.shape[0] * groups * length)
    sent, residue_grad, decay_grad = pl.pallas_call(
        lambda *refs: total_kernel(factor, *refs),
        out_shape=(shape(blocks, CARRY_ROWS, LANES, dtype=BF16), flip, flip),
        compiler_params=small_params,
        name="total",
    )(message, carry.transpose(1, 0, 2))
    carry = lax.all_to_all(sent, "seq", 0, 0, tiled=True)

    names = ("carried",)
    *outs, filter_grad = pl.pallas_call(
        finish_kernel,
        grid=grid,
        in_specs=[tall, filters, flat(8), flat(8)] + [flat(BLOCK)] * 4
        + [chunks(CARRY_ROWS)] + table_specs(names),
        out_specs=[tall] * 3 + [filters],
        out_shape=[jax.ShapeDtypeStruct(query_rows.shape, BF16)] * 3 + [shape(3, 3, width)],
        compiler_params=params,
        name="finish",
    )(
        cotangent, short_filter, after, local_edge, key_short, value_short,
        mixed, grad, carry, *[tables[name] for name in names],
    )
    return (*outs, filter_grad, residue_grad.T, decay_grad.T)


def solution(mesh):
    rows = P("dp", "seq", None)
    return jax.shard_map(
        body,
        mesh=mesh,
        in_specs=(rows, rows, rows, rows, P(), P("seq", None), P("seq", None)),
        out_specs=(rows, rows, rows, P(), P("seq", None), P("seq", None)),
        check_vma=False,
    )
```
